512 devices in a mesh: tok: 32 (over z, core), col: 16 (over x, y).
Axes of the slice: x: 4, y: 4, z: 16, core: 2. Of those that a mesh axis runs over, the one named last changes fastest.
Arguments:
- tokens: bfloat16 [24576, 2048], P('tok', 'col'), may hold values from -6 to 6
- cotangent: bfloat16 [24576, 2048], P('tok', 'col'), may hold values from -6 to 6
- query_weight: bfloat16 [2048, 2048], P(None, 'col'), may hold values from -1 to 1
- slot_keys: bfloat16 [32768, 2048], P('tok', 'col'), may hold values from -64 to 64
- values: float32 [32768, 2048], P('tok', 'col'), may hold values from -6 to 6
- momentum: float32 [32768, 2048], P('tok', 'col'), may hold values from -0.3 to 0.3
- page_ids: int32 [384, 4], P('tok'), may hold values from 0 to 255, as said below
- last_step: int32 [256], P('tok'), may hold values from 0 to 63
- decay_rate: float32 [2048], P('col'), may hold values from 0.004 to 0.08
- gate_weight: bfloat16 [2048, 2048], P(None, 'col'), may hold values from -0.125 to 0.125
- out_weight: bfloat16 [2048, 2048], P('col'), may hold values from -0.1875 to 0.1875
Outputs:
- layer_out: bfloat16 [24576, 2048], P('tok', 'col')
- new_values: float32 [32768, 2048], P('tok', 'col')
- new_momentum: float32 [32768, 2048], P('tok', 'col')
The draws below stay inside these ranges and needn't reach their ends.
Inputs may be any that keep to these rules, and one draw needn't show every extreme that they name: `page_ids`: page p belongs to owner group p // 8. Among the 48 pages listed by the blocks of one index of tok, counted with repeats, at most 2 belong to any one owner group, and one owner group gets exactly 2 from every index of tok. A block may list a page more than once.
All inputs are finite; a program needn't handle non-finite values.
Results may differ from the reference program's by a relative error of at most 0.014.
Values may be sent and summed in bfloat16 or wider, within the bound.
A program may use at most 64 MiB of HBM per device.

```python
import math
import jax
import jax.numpy as jnp
from jax import lax

D = 2048
KW = 2048
PAGE = 128
PICKS = 4
BLK = 64
STEP = 64
NB = 12
PAGES_DEV = 8
TOKENS = 24576
NBLOCKS = 384
PAGES = 256
SLOTS = 32768
CAP = 2
N_COL = 16


def page_table(key):
    base_key = jax.random.fold_in(key, 101)
    sources = PAGES // PAGES_DEV
    slots_all = sources * CAP
    skipped = max(1, PAGES_DEV // 4)
    usable = PAGES_DEV - skipped
    hot_owner = jax.random.randint(jax.random.fold_in(base_key, 1), (), 0, sources)
    owner_pool = (jnp.arange(slots_all) // CAP).astype(jnp.int32)

    def group_order(group):
        return jax.random.permutation(jax.random.fold_in(base_key, group + 5000), PAGES_DEV).astype(jnp.int32)
    orders = jax.vmap(group_order)(jnp.arange(sources))

    def one_source(source):
        source_key = jax.random.fold_in(base_key, source + 7)
        shuffled = jax.random.permutation(jax.random.fold_in(source_key, 1), slots_all).astype(jnp.int32)
        priority = jnp.where(owner_pool == hot_owner, 0, 1) * slots_all + shuffled
        ordering = jnp.argsort(priority, stable=True)
        chosen = owner_pool[ordering][:PICKS * NB]
        chosen = jax.random.permutation(jax.random.fold_in(source_key, 2), chosen)
        within = jax.random.randint(jax.random.fold_in(source_key, 3), (PICKS * NB,), 0, usable)
        in_group = orders[chosen, within]
        return (chosen * PAGES_DEV + in_group).reshape(NB, PICKS)
    return jax.vmap(one_source)(jnp.arange(sources)).reshape(NB * sources, PICKS).astype(jnp.int32)


def token_table(key):
    return jnp.clip(jax.random.normal(jax.random.fold_in(key, 202), (TOKENS, D), jnp.float32), -6.0, 6.0)


def query_table(key):
    return jnp.clip(jax.random.normal(jax.random.fold_in(key, 303), (D, KW), jnp.float32), -6.0, 6.0) / math.sqrt(D)


def draw_tokens(key, part):
    return token_table(key).astype(jnp.bfloat16)


def draw_query_weight(key, part):
    return query_table(key).astype(jnp.bfloat16)


def draw_page_ids(key, part):
    return page_table(key)


def draw_slot_keys(key, part):
    drawn = jnp.clip(jax.random.normal(jax.random.fold_in(key, 404), (SLOTS, KW), jnp.float32), -6.0, 6.0)
    return drawn.astype(jnp.bfloat16)


def with_ends(values, rng, low, largest):
    dims = values.shape
    spot = [jax.random.randint(jax.random.fold_in(rng, axis), (), 0, dims[axis]) for axis in range(len(dims))]
    values = values.at[tuple(spot)].set(low)
    longest = dims.index(max(dims))
    spot[longest] = (spot[longest] + 1) % dims[longest]
    return values.at[tuple(spot)].set(largest)


def raised(values, stream_key, source, target, parts, factor):
    def block_of(position):
        return (jnp.arange(values.shape[position]) // (values.shape[position] // parts)).reshape((-1,) + (1,) * (values.ndim - 1 - position))

    first = jax.random.permutation(stream_key, parts)[block_of(target)]
    far = (block_of(target) + parts // 2) % parts
    return jnp.where((block_of(source) == first) | (block_of(source) == far), factor * values, values)


def steps_of(own_key, extent, pieces, low, largest):
    level, own = 1.0, jax.random.fold_in(own_key, 6)
    for dim, parts in pieces:
        draws = jnp.exp(jax.random.uniform(jax.random.fold_in(own, dim), (parts,), jnp.float32, low / len(pieces), largest / len(pieces)))
        level = level * jnp.repeat(draws, extent[dim] // parts).reshape([-1 if axis == dim else 1 for axis in range(len(extent))])
    return level


def noise(stream_key, shape, scale, bound, cuts=(), kind=jnp.bfloat16):
    loudness = steps_of(stream_key, shape, cuts, -0.22, 0.18) if cuts else 1.0
    result = jax.random.normal(stream_key, shape, jnp.float32) * scale * loudness
    return jnp.minimum(jnp.maximum(result, -bound), bound).astype(kind)


def noise_with(key, dims, scale, most, split, heavy, dtype=jnp.bfloat16):
    values = scale * jax.random.normal(key, dims, jnp.float32)
    if split:
        values = values * steps_of(key, dims, split, -0.22, 0.18)
    return jnp.clip(raised(values, jax.random.fold_in(key, 3), *heavy), -most, most).astype(dtype)


def setup_inputs(seed: int = 0) -> dict:
    streams_of = jax.random.split(jax.random.key(seed), 12)
    return {
        "tokens": draw_tokens(jax.random.fold_in(streams_of[11], 71), 0),
        "cotangent": noise(streams_of[1], (TOKENS, D), 1.0, 6.0, ((0, 32), (1, 16))),
        "query_weight": draw_query_weight(jax.random.fold_in(streams_of[11], 71), 0),
        "slot_keys": draw_slot_keys(jax.random.fold_in(streams_of[11], 71), 0),
        "values": noise(streams_of[4], (SLOTS, D), 1.0, 6.0, ((0, 32), (1, 16)), jnp.float32),
        "momentum": noise(streams_of[5], (SLOTS, D), 0.05, 0.3, ((0, 32), (1, 16)), jnp.float32),
        "page_ids": draw_page_ids(jax.random.fold_in(streams_of[11], 71), 0),
        "last_step": with_ends(jax.random.randint(streams_of[7], (PAGES,), 0, STEP), jax.random.fold_in(streams_of[7], 1), 0, STEP - 1).astype(jnp.int32),
        "decay_rate": jnp.clip(jnp.exp(math.log(0.08) - 2.9957322 * jax.random.uniform(streams_of[8], (D,), jnp.float32) ** steps_of(streams_of[8], (D,), ((0, 16),), -0.2, 0.2)), 0.004, 0.08),
        "gate_weight": noise(streams_of[9], (D, D), D ** -0.5, 0.125, ((1, 16),)),
        "out_weight": noise_with(streams_of[10], (D, D), D ** -0.5, 0.1875, ((0, 16),), (0, 1, 16, 2.0)),
    }


MOMENTUM_RATE = 0.9
LEARN_RATE = 1.0


def reference(tokens, cotangent, query_weight, slot_keys, values, momentum, page_ids, last_step, decay_rate, gate_weight, out_weight):
    elapsed = (STEP - last_step).astype(jnp.float32)
    factor = jnp.exp(-elapsed[:, None] * decay_rate[None, :])
    stored = values.reshape(PAGES, PAGE, D)
    decayed = (stored * factor[:, None, :]).astype(jnp.bfloat16)
    key_pages = slot_keys.reshape(PAGES, PAGE, KW)
    queries = jnp.dot(tokens, query_weight, preferred_element_type=jnp.float32).astype(jnp.bfloat16)
    query_blocks = queries.reshape(NBLOCKS, BLK, KW)

    def lookup(block_args):
        block_queries, listed = block_args
        block_keys = key_pages[listed].reshape(PICKS * PAGE, KW)
        block_values = decayed[listed].reshape(PICKS * PAGE, D)
        scores = jnp.dot(block_queries, block_keys.T, preferred_element_type=jnp.float32) * (KW ** -0.5)
        weights = jax.nn.softmax(scores, axis=-1).astype(jnp.bfloat16)
        return weights, jnp.dot(weights, block_values, preferred_element_type=jnp.float32)

    weights, memory = lax.map(lookup, (query_blocks, page_ids))
    memory = memory.reshape(TOKENS, D)
    gate_logits = jnp.dot(tokens, gate_weight, preferred_element_type=jnp.float32)
    activation = jax.nn.silu(gate_logits)
    gated_memory = (memory * activation).astype(jnp.bfloat16)
    shard_width = D // N_COL

    def add_shard(shard_index, running):
        first_col = (shard_index * shard_width).astype(jnp.int32)
        gated_piece = lax.dynamic_slice_in_dim(gated_memory, first_col, shard_width, 1)
        weight_rows = lax.dynamic_slice_in_dim(out_weight, first_col, shard_width, 0)
        partial_value = jnp.dot(gated_piece, weight_rows, preferred_element_type=jnp.float32).astype(jnp.bfloat16)
        partial_value = lax.optimization_barrier(partial_value)
        return running + partial_value.astype(jnp.float32)

    layer_out = lax.fori_loop(0, N_COL, add_shard, jnp.zeros((TOKENS, D), jnp.float32)).astype(jnp.bfloat16)

    grad_gated = jnp.dot(cotangent, out_weight.T, preferred_element_type=jnp.float32)
    grad_memory = (grad_gated * activation).astype(jnp.bfloat16).reshape(NBLOCKS, BLK, D)

    def accumulate(running_grad, block_args):
        block_weights, block_grad, listed = block_args
        slot_grad = jnp.dot(block_weights.T, block_grad, preferred_element_type=jnp.float32).astype(jnp.bfloat16)
        running_grad = running_grad.at[listed].add(slot_grad.astype(jnp.float32).reshape(PICKS, PAGE, D))
        return running_grad, None

    page_grad, unused = lax.scan(accumulate, jnp.zeros((PAGES, PAGE, D), jnp.float32), (weights, grad_memory, page_ids))
    touched = jnp.zeros((PAGES,), jnp.float32).at[page_ids.reshape(-1)].add(1.0) > 0.0
    touch_mask = touched[:, None, None]
    moment = momentum.reshape(PAGES, PAGE, D)
    new_momentum = jnp.where(touch_mask, MOMENTUM_RATE * moment + page_grad * factor[:, None, :], moment)
    new_values = jnp.where(touch_mask, stored * factor[:, None, :] - LEARN_RATE * new_momentum, stored)
    return layer_out, new_values.reshape(SLOTS, D), new_momentum.reshape(SLOTS, D)
```

```python
import jax
import jax.numpy as jnp
from jax import lax
from jax.experimental import pallas as pl
from jax.experimental.pallas import tpu as pltpu
from jax.sharding import PartitionSpec as P

KW = 2048
STEP = 64
MOMENTUM_RATE = 0.9
LEARN_RATE = 1.0

NZ = 16
NX = 4
NCOL = 16
ROWS = 768
NB = 12
PICKS = 4
BLK = 64
PAGE = 128
LANE = 128
OWN = 1024
SHARE = ROWS // NCOL
LIST = PICKS * PAGE
HALF = ROWS // 2
CNT = 16
GROWS = OWN + CNT
MESH = pl.DeviceIdType.MESH
HOPS = ((8, 7), (7, 8))
ANY = pl.BlockSpec(memory_space=pl.ANY)
VM = pl.BlockSpec(memory_space=pltpu.VMEM)
SM = pl.BlockSpec(memory_space=pltpu.SMEM)


class Place:
    def __init__(self):
        self.tok = lax.axis_index("tok")
        self.col = lax.axis_index("col")
        self.z = self.tok // 2
        self.c = self.tok % 2
        self.x = self.col // NX
        self.y = self.col % NX
        self.sib = (self.zc(0, 1 - self.c), self.col)
        self.zn = ((self.zc(1, self.c), self.col), (self.zc(-1, self.c), self.col))

    def zc(self, dz, c):
        return ((self.z + dz + NZ) % NZ) * 2 + c

    def xy(self, dx, dy):
        return ((self.x + dx + NX) % NX) * NX + (self.y + dy + NX) % NX

    def peer(self, dx, dy):
        return (self.tok, self.xy(dx, dy))


def remote(src, dst, ssem, rsem, dev):
    return pltpu.make_async_remote_copy(
        src_ref=src, dst_ref=dst, send_sem=ssem, recv_sem=rsem, device_id=dev, device_id_type=MESH
    )


def greet(devices):
    barrier = pltpu.get_barrier_semaphore()
    for dev in devices:
        pl.semaphore_signal(barrier, inc=1, device_id=dev, device_id_type=MESH)
    pl.semaphore_wait(barrier, len(devices))


def z_gather(at, src, dst, rsend, rrecv, ssend, srecv, own):
    half = OWN // 2
    sent = []

    def start(copy):
        copy.start()
        sent.append(copy)

    for d in range(2):
        for h in range(2):
            rows = pl.ds(h * half, half)
            start(remote(src.at[rows], dst.at[at.tok, rows], rsend.at[d, h, 0], rrecv.at[d, h, 0], at.zn[d]))
    start(remote(src, dst.at[at.tok], own.at[0], own.at[1], at.sib))
    local = pltpu.make_async_copy(src, dst.at[at.tok], own.at[2])
    local.start()
    yield
    for s in range(1, 9):
        for d in range(2):
            for h in range(2):
                if s > HOPS[d][h]:
                    continue
                rows = pl.ds(h * half, half)
                block = dst.at[at.zc(-s if d == 0 else s, at.c), rows]
                remote(block, block, rsend.at[d, h, s - 1], rrecv.at[d, h, s - 1], at.zn[d]).wait_recv()
                if s < HOPS[d][h]:
                    start(remote(block, block, rsend.at[d, h, s], rrecv.at[d, h, s], at.zn[d]))
                start(remote(block, block, ssend.at[d, h, s - 1], srecv.at[d, h, s - 1], at.sib))
        yield
    mine = dst.at[at.zc(0, 1 - at.c)]
    remote(mine, mine, own.at[0], own.at[1], at.sib).wait_recv()
    for d in range(2):
        for h in range(2):
            for s in range(1, HOPS[d][h] + 1):
                rows = pl.ds(h * half, half)
                block = dst.at[at.zc(-s if d == 0 else s, 1 - at.c), rows]
                remote(block, block, ssend.at[d, h, s - 1], srecv.at[d, h, s - 1], at.sib).wait_recv()
    for copy in sent:
        copy.wait_send()
    local.wait()
    yield


def xy_gather(at, src, dst, sends, recvs, local_sem, first):
    sent = []
    lo, hi = pl.ds(0, HALF), pl.ds(HALF, HALF)

    def shift(a, b):
        return (a, b) if first == 0 else (b, a)

    def dev(a, b):
        return at.peer(*shift(a, b))

    def slot(a, b):
        return dst.at[at.xy(*shift(a, b))]

    def start(block, k, to):
        copy = remote(block, block, sends.at[k], recvs.at[k], to)
        copy.start()
        sent.append(copy)

    def wait(block, k, to):
        remote(block, block, sends.at[k], recvs.at[k], to).wait_recv()

    for k, a in ((0, 1), (1, -1)):
        copy = remote(src, slot(0, 0), sends.at[k], recvs.at[k], dev(a, 0))
        copy.start()
        sent.append(copy)
    for k, b in ((4, 1), (5, -1)):
        copy = remote(src, slot(0, 0), sends.at[k], recvs.at[k], dev(0, b))
        copy.start()
        sent.append(copy)
    local = pltpu.make_async_copy(src, slot(0, 0), local_sem)
    local.start()
    yield
    wait(slot(-1, 0), 0, dev(1, 0))
    start(slot(-1, 0).at[lo], 2, dev(1, 0))
    wait(slot(1, 0), 1, dev(-1, 0))
    start(slot(1, 0).at[hi], 3, dev(-1, 0))
    for item, a in ((1, -1), (2, 1)):
        start(slot(a, 0), 4 + 4 * item, dev(0, 1))
        start(slot(a, 0), 5 + 4 * item, dev(0, -1))
    yield
    wait(slot(2, 0).at[lo], 2, dev(1, 0))
    wait(slot(2, 0).at[hi], 3, dev(-1, 0))
    start(slot(2, 0), 4 + 4 * 3, dev(0, 1))
    start(slot(2, 0), 5 + 4 * 3, dev(0, -1))
    yield
    for item, a in ((0, 0), (1, -1), (2, 1), (3, 2)):
        k = 4 + 4 * item
        wait(slot(a, -1), k, dev(0, 1))
        start(slot(a, -1).at[lo], k + 2, dev(0, 1))
        wait(slot(a, 1), k + 1, dev(0, -1))
        start(slot(a, 1).at[hi], k + 3, dev(0, -1))
        yield
    for item, a in ((0, 0), (1, -1), (2, 1), (3, 2)):
        k = 4 + 4 * item
        wait(slot(a, 2).at[lo], k + 2, dev(0, 1))
        wait(slot(a, 2).at[hi], k + 3, dev(0, -1))
    for copy in sent:
        copy.wait_send()
    local.wait()
    yield


def together(*parts):
    parts = list(parts)
    while parts:
        alive = []
        for part in parts:
            try:
                next(part)
                alive.append(part)
            except StopIteration:
                pass
        parts = alive


def dma(*shape):
    return pltpu.SemaphoreType.DMA(shape)


Z_SEMS = [dma(2, 2, 8), dma(2, 2, 8), dma(2, 2, 8), dma(2, 2, 8), dma(3)]


def params(ident, vmem=56 << 20):
    return pltpu.CompilerParams(collective_id=ident, has_side_effects=True, vmem_limit_bytes=vmem)


def gather_kernel(keys, tokens, cotangent, kall, tall, call, *sems):
    at = Place()
    greet([at.zn[0], at.zn[1], at.sib, at.peer(1, 0), at.peer(-1, 0), at.peer(0, 1), at.peer(0, -1)])
    together(
        z_gather(at, keys, kall, *sems[:5]),
        xy_gather(at, tokens, tall, sems[5], sems[6], sems[9].at[0], 0),
        xy_gather(at, cotangent, call, sems[7], sems[8], sems[9].at[1], 1),
    )


def gather(keys, tokens, cotangent):
    blocks = jax.ShapeDtypeStruct((NCOL, ROWS, LANE), jnp.bfloat16)
    return pl.pallas_call(
        gather_kernel,
        out_shape=(jax.ShapeDtypeStruct((2 * NZ, OWN, LANE), jnp.bfloat16), blocks, blocks),
        in_specs=[ANY] * 3,
        out_specs=(ANY,) * 3,
        scratch_shapes=Z_SEMS + [dma(20), dma(20), dma(20), dma(20), dma(2)],
        compiler_params=params(0),
    )(keys, tokens, cotangent)


def fetch_pages(pids, pages, buf, sem):
    copies = []
    for n in range(NB * PICKS):
        copy = pltpu.make_async_copy(pages.at[pids[n // PICKS, n % PICKS]], buf.at[n], sem.at[n])
        copy.start()
        copies.append(copy)
    return copies


def project_kernel(pids, tall, call, wq, wg, wo, pages, scores, act, grads, qbuf, kbuf, sem):
    copies = fetch_pages(pids, pages, kbuf, sem)
    tile = 128

    def step(r, carry):
        rows = pl.ds(pl.multiple_of(r * tile, tile), tile)
        qs = jnp.zeros((tile, LANE), jnp.float32)
        gs = jnp.zeros((tile, LANE), jnp.float32)
        cs = jnp.zeros((tile, LANE), jnp.float32)
        for k in range(NCOL):
            t = tall[k, rows, :]
            qs += jnp.dot(t, wq[k], preferred_element_type=jnp.float32)
            gs += jnp.dot(t, wg[k], preferred_element_type=jnp.float32)
            cs += lax.dot_general(
                call[k, rows, :],
                wo[:, k * LANE : (k + 1) * LANE],
                (((1,), (1,)), ((), ())),
                preferred_element_type=jnp.float32,
            )
        a = gs / (1.0 + jnp.exp(-gs))
        act[rows, :] = a
        grads[rows, :] = (cs * a).astype(jnp.bfloat16)
        qbuf[rows, :] = qs.astype(jnp.bfloat16)
        return carry

    lax.fori_loop(0, ROWS // tile, step, 0)
    for copy in copies:
        copy.wait()

    def block(b, carry):
        rows = pl.ds(pl.multiple_of(b * BLK, BLK), BLK)
        q = qbuf[rows, :]
        for i in range(PICKS):
            scores[rows, i * PAGE : (i + 1) * PAGE] = lax.dot_general(
                q, kbuf[b * PICKS + i], (((1,), (1,)), ((), ())), preferred_element_type=jnp.float32
            )
        return carry

    lax.fori_loop(0, NB, block, 0)


def project(pids, tall, call, wq, wg, wo, pages):
    return pl.pallas_call(
        project_kernel,
        out_shape=(
            jax.ShapeDtypeStruct((ROWS, LIST), jnp.float32),
            jax.ShapeDtypeStruct((ROWS, LANE), jnp.float32),
            jax.ShapeDtypeStruct((ROWS, LANE), jnp.bfloat16),
        ),
        in_specs=[SM] + [VM] * 5 + [ANY],
        out_specs=(VM,) * 3,
        scratch_shapes=[
            pltpu.VMEM((ROWS, LANE), jnp.bfloat16),
            pltpu.VMEM((NB * PICKS, PAGE, LANE), jnp.bfloat16),
            dma(NB * PICKS),
        ],
        compiler_params=pltpu.CompilerParams(vmem_limit_bytes=56 << 20),
    )(pids, tall, call, wq, wg, wo, pages)


def peers(at):
    return [(dx, dy) for dx in (0, 1, -1, 2) for dy in (0, 1, -1, 2) if (dx, dy) != (0, 0)]


def weigh(at, scores, weights, got, share, wsend, wrecv, ssend, srecv):
    around = peers(at)
    sent = []
    for k, (dx, dy) in enumerate(around):
        to = at.xy(dx, dy)
        copy = remote(scores.at[to], got.at[k], ssend.at[k], srecv.at[k], at.peer(dx, dy))
        copy.start()
        sent.append(copy)
    for _ in range(5):
        yield
    for k, (dx, dy) in enumerate(around):
        remote(got.at[k], got.at[k], ssend.at[k], srecv.at[k], at.peer(dx, dy)).wait_recv()
    total = scores[at.col]
    for k in range(len(around)):
        total = total + got[k]
    total = total * (KW**-0.5)
    e = jnp.exp(total - jnp.max(total, axis=1, keepdims=True))
    w = (e / jnp.sum(e, axis=1, keepdims=True)).astype(jnp.bfloat16)
    share[...] = w
    weights[at.col] = w
    for k, (dx, dy) in enumerate(around):
        copy = remote(share, weights.at[at.col], wsend.at[k], wrecv.at[k], at.peer(dx, dy))
        copy.start()
        sent.append(copy)
    yield
    yield
    yield
    for k, (dx, dy) in enumerate(around):
        block = weights.at[at.xy(-dx, -dy)]
        remote(block, block, wsend.at[k], wrecv.at[k], at.peer(dx, dy)).wait_recv()
    for copy in sent:
        copy.wait_send()
    yield


def weigh_kernel(stored, scores, vall, wout, got, share, weights, *sems):
    at = Place()
    greet([at.zn[0], at.zn[1], at.sib] + [at.peer(dx, dy) for dx, dy in peers(at)])
    together(
        z_gather(at, stored, vall, *sems[:5]),
        weigh(at, scores, weights, got, share, *sems[5:]),
    )
    wout[...] = weights[...]


def weigh_call(stored, scores):
    return pl.pallas_call(
        weigh_kernel,
        out_shape=(
            jax.ShapeDtypeStruct((2 * NZ, OWN, LANE), jnp.bfloat16),
            jax.ShapeDtypeStruct((NCOL, SHARE, LIST), jnp.bfloat16),
        ),
        in_specs=[ANY, VM],
        out_specs=(ANY, VM),
        scratch_shapes=[
            pltpu.VMEM((NCOL - 1, SHARE, LIST), jnp.float32),
            pltpu.VMEM((SHARE, LIST), jnp.bfloat16),
            pltpu.VMEM((NCOL, SHARE, LIST), jnp.bfloat16),
        ]
        + Z_SEMS
        + [dma(15)] * 4,
        compiler_params=params(1),
    )(stored, scores)


def mix_kernel(pids, weights, act, grads, wo, pages, outa, outb, acc, gated, vbuf, sem):
    copies = fetch_pages(pids, pages, vbuf, sem)

    def clear(n, carry):
        acc[n] = jnp.zeros((GROWS, LANE), jnp.bfloat16)
        return carry

    lax.fori_loop(0, 2 * NZ, clear, 0)
    row = lax.broadcasted_iota(jnp.int32, (2 * NZ, CNT, LANE), 1)
    page = lax.broadcasted_iota(jnp.int32, (2 * NZ, CNT, LANE), 0) * 8 + row
    page = jnp.where(row < 8, page, -1)
    count = jnp.zeros((2 * NZ, CNT, LANE), jnp.float32)
    for n in range(NB * PICKS):
        count += jnp.where(page == pids[n // PICKS, n % PICKS], 1.0, 0.0)
    acc[:, OWN:, :] = count.astype(jnp.bfloat16)

    def grad(b, carry):
        rows = pl.ds(pl.multiple_of(b * BLK, BLK), BLK)
        g = grads[rows, :]
        for i in range(PICKS):
            w = weights[rows, i * PAGE : (i + 1) * PAGE]
            s = lax.dot_general(w, g, (((0,), (0,)), ((), ())), preferred_element_type=jnp.float32)
            p = pids[b, i]
            at = (p // 8, pl.ds(pl.multiple_of((p % 8) * PAGE, PAGE), PAGE))
            acc[at] = (acc[at].astype(jnp.float32) + s).astype(jnp.bfloat16)
        return carry

    lax.fori_loop(0, NB, grad, 0)
    for copy in copies:
        copy.wait()

    def block(b, carry):
        rows = pl.ds(pl.multiple_of(b * BLK, BLK), BLK)
        m = jnp.zeros((BLK, LANE), jnp.float32)
        for i in range(PICKS):
            m += jnp.dot(
                weights[rows, i * PAGE : (i + 1) * PAGE],
                vbuf[b * PICKS + i],
                preferred_element_type=jnp.float32,
            )
        gated[rows, :] = (m * act[rows, :]).astype(jnp.bfloat16)
        return carry

    lax.fori_loop(0, NB, block, 0)
    for k in range(NCOL):
        o = jnp.dot(
            gated[...], wo[:, k * LANE : (k + 1) * LANE], preferred_element_type=jnp.float32
        ).astype(jnp.bfloat16)
        outa[k] = o[:HALF]
        outb[(k % NX) * NX + k // NX] = o[HALF:]


def mix(pids, weights, act, grads, wo, pages):
    halves = jax.ShapeDtypeStruct((NCOL, HALF, LANE), jnp.bfloat16)
    return pl.pallas_call(
        mix_kernel,
        out_shape=(halves, halves, jax.ShapeDtypeStruct((2 * NZ, GROWS, LANE), jnp.bfloat16)),
        in_specs=[SM] + [VM] * 4 + [ANY],
        out_specs=(VM,) * 3,
        scratch_shapes=[
            pltpu.VMEM((ROWS, LANE), jnp.bfloat16),
            pltpu.VMEM((NB * PICKS, PAGE, LANE), jnp.bfloat16),
            dma(NB * PICKS),
        ],
        compiler_params=pltpu.CompilerParams(vmem_limit_bytes=56 << 20),
    )(pids, weights, act, grads, wo, pages)


def sub(h):
    return (0, 528, 176) if h == 0 else (528, 512, 128)


def z_reduce(at, mine, total, theirs, stage, land, xsend, xrecv, rsend, rrecv):
    sent = []
    for n, off in enumerate((8, 7, -7, 6, -6, 5, -5, 4, -4, 3, -3, 2, -2, 1, -1, 0)):
        copy = remote(
            mine.at[at.zc(off, 1 - at.c)], theirs.at[off + 7], xsend.at[off + 7], xrecv.at[off + 7], at.sib
        )
        copy.start()
        sent.append(copy)

    def wait_sib(off):
        block = theirs.at[off + 7]
        remote(block, block, xsend.at[off + 7], xrecv.at[off + 7], at.sib).wait_recv()

    def landed(d, h, s):
        first, size, tile = sub(h)
        block = land.at[d, s, pl.ds(first, size)]
        remote(block, block, rsend.at[d, h, s], rrecv.at[d, h, s], at.zn[d]).wait_recv()

    wait_sib(8)
    for s in range(8):
        if s < 7:
            wait_sib(7 - s)
            wait_sib(s - 7)
        for d in range(2):
            for h in range(2):
                if s >= HOPS[d][h]:
                    continue
                far = HOPS[d][h] - s
                off = far if d == 0 else -far
                buf = 8 if far == 8 else off
                owner = at.zc(off, at.c)
                first, size, tile = sub(h)
                if s:
                    landed(d, h, s - 1)
                for t in range(size // tile):
                    rows = pl.ds(first + t * tile, tile)
                    v = mine[owner, rows, :].astype(jnp.float32) + theirs[buf + 7, rows, :].astype(jnp.float32)
                    if s:
                        v = v + land[d, s - 1, rows, :].astype(jnp.float32)
                    stage[d, s, rows, :] = v.astype(jnp.bfloat16)
                rows = pl.ds(first, size)
                copy = remote(
                    stage.at[d, s, rows], land.at[d, s, rows], rsend.at[d, h, s], rrecv.at[d, h, s], at.zn[d]
                )
                copy.start()
                sent.append(copy)
        yield
    wait_sib(0)
    for h in range(2):
        first, size, tile = sub(h)
        for d in range(2):
            landed(d, h, HOPS[d][h] - 1)
        for t in range(size // tile):
            rows = pl.ds(first + t * tile, tile)
            v = mine[at.tok, rows, :].astype(jnp.float32) + theirs[7, rows, :].astype(jnp.float32)
            for d in range(2):
                v = v + land[d, HOPS[d][h] - 1, rows, :].astype(jnp.float32)
            total[rows, :] = v
    for copy in sent:
        copy.wait_send()
    yield


def xy_reduce(at, terms, out, first, got1, part, got2, send1, recv1, send2, recv2):
    sent = []
    mine = (at.x, at.y) if first == 0 else (at.y, at.x)

    def dev(a, b):
        return at.peer(a, b) if first == 0 else at.peer(b, a)

    for k, a in enumerate((2, 1, -1)):
        line = (mine[0] + a + NX) % NX
        copy = remote(terms.at[pl.ds(line * NX, NX)], got1.at[k], send1.at[k], recv1.at[k], dev(a, 0))
        copy.start()
        sent.append(copy)
    for _ in range(4):
        yield
    for k, a in enumerate((2, 1, -1)):
        remote(got1.at[k], got1.at[k], send1.at[k], recv1.at[k], dev(a, 0)).wait_recv()
    for b in range(NX):
        v = terms[mine[0] * NX + b].astype(jnp.float32)
        for k in range(3):
            v = v + got1[k, b].astype(jnp.float32)
        part[b] = v.astype(jnp.bfloat16)
    for k, b in enumerate((2, 1, -1)):
        copy = remote(part.at[(mine[1] + b + NX) % NX], got2.at[k], send2.at[k], recv2.at[k], dev(0, b))
        copy.start()
        sent.append(copy)
    yield
    yield
    for k, b in enumerate((2, 1, -1)):
        remote(got2.at[k], got2.at[k], send2.at[k], recv2.at[k], dev(0, b)).wait_recv()
    v = part[mine[1]].astype(jnp.float32)
    for k in range(3):
        v = v + got2[k].astype(jnp.float32)
    out[pl.ds(first * HALF, HALF), :] = v.astype(jnp.bfloat16)
    for copy in sent:
        copy.wait_send()
    yield


def reduce_kernel(outa, outb, acc, out, total, *rest):
    at = Place()
    greet(
        [at.zn[0], at.zn[1], at.sib]
        + [at.peer(a, 0) for a in (1, -1, 2)]
        + [at.peer(0, a) for a in (1, -1, 2)]
    )
    together(
        xy_reduce(at, outa, out, 0, *rest[:7]),
        xy_reduce(at, outb, out, 1, *rest[7:14]),
        z_reduce(at, acc, total, *rest[14:]),
    )


def reduce_call(outa, outb, acc):
    xy = [
        pltpu.VMEM((3, NX, HALF, LANE), jnp.bfloat16),
        pltpu.VMEM((NX, HALF, LANE), jnp.bfloat16),
        pltpu.VMEM((3, HALF, LANE), jnp.bfloat16),
    ] + [dma(3)] * 4
    return pl.pallas_call(
        reduce_kernel,
        out_shape=(
            jax.ShapeDtypeStruct((ROWS, LANE), jnp.bfloat16),
            jax.ShapeDtypeStruct((GROWS, LANE), jnp.float32),
        ),
        in_specs=[VM] * 3,
        out_specs=(VM,) * 2,
        scratch_shapes=xy
        + xy
        + [
            pltpu.VMEM((NZ, GROWS, LANE), jnp.bfloat16),
            pltpu.VMEM((2, 8, GROWS, LANE), jnp.bfloat16),
            pltpu.VMEM((2, 8, GROWS, LANE), jnp.bfloat16),
            dma(16),
            dma(16),
            dma(2, 2, 8),
            dma(2, 2, 8),
        ],
        compiler_params=params(2),
    )(outa, outb, acc)


def per_device(
    tokens,
    cotangent,
    query_weight,
    slot_keys,
    values,
    momentum,
    page_ids,
    last_step,
    decay_rate,
    gate_weight,
    out_weight,
):
    pages_local = last_step.shape[0]
    elapsed = (STEP - last_step).astype(jnp.float32)
    factor = jnp.exp(-elapsed[:, None] * decay_rate[None, :])[:, None, :]
    stored = values.reshape(pages_local, PAGE, LANE)
    decayed = (stored * factor).astype(jnp.bfloat16).reshape(OWN, LANE)
    kall, tall, call = gather(slot_keys, tokens, cotangent)
    scores, act, grads = project(
        page_ids,
        tall,
        call,
        query_weight.reshape(NCOL, LANE, LANE),
        gate_weight.reshape(NCOL, LANE, LANE),
        out_weight,
        kall.reshape(-1, PAGE, LANE),
    )
    vall, weights = weigh_call(decayed, scores.reshape(NCOL, SHARE, LIST))
    outa, outb, acc = mix(
        page_ids, weights.reshape(ROWS, LIST), act, grads, out_weight, vall.reshape(-1, PAGE, LANE)
    )
    layer_out, total = reduce_call(outa, outb, acc)
    page_grad = total[:OWN].reshape(pages_local, PAGE, LANE)
    touched = (total[OWN : OWN + pages_local, 0] > 0.5)[:, None, None]
    moment = momentum.reshape(pages_local, PAGE, LANE)
    new_momentum = jnp.where(touched, MOMENTUM_RATE * moment + page_grad * factor, moment)
    new_values = jnp.where(touched, stored * factor - LEARN_RATE * new_momentum, stored)
    return (layer_out, new_values.reshape(OWN, LANE), new_momentum.reshape(OWN, LANE))


def solution(mesh):
    in_specs = (
        P("tok", "col"),
        P("tok", "col"),
        P(None, "col"),
        P("tok", "col"),
        P("tok", "col"),
        P("tok", "col"),
        P("tok", None),
        P("tok"),
        P("col"),
        P(None, "col"),
        P("col", None),
    )
    out_specs = (P("tok", "col"), P("tok", "col"), P("tok", "col"))
    return jax.shard_map(
        per_device, mesh=mesh, in_specs=in_specs, out_specs=out_specs, check_vma=False
    )
```

```python
import jax
import jax.numpy as jnp
from jax import lax
from jax.experimental import pallas as pl
from jax.experimental.pallas import tpu as pltpu
from jax.sharding import PartitionSpec as P

KW = 2048
STEP = 64
MOMENTUM_RATE = 0.9
LEARN_RATE = 1.0

NZ = 16
NX = 4
NCOL = 16
ROWS = 768
NB = 12
PICKS = 4
PAIRS = NB * PICKS
BLK = 64
PAGE = 128
LANE = 128
LOCAL = 8
OWNERS = 2 * NZ
PAGES = OWNERS * LOCAL
OWN = 1024
SHARE = ROWS // NCOL
HALF = ROWS // 2
CNT = 16
GROWS = OWN + CNT
MESH = pl.DeviceIdType.MESH
HOPS = ((8, 7), (7, 8))
VM = pl.BlockSpec(memory_space=pltpu.VMEM)
SM = pl.BlockSpec(memory_space=pltpu.SMEM)
F32 = jnp.float32
BF16 = jnp.bfloat16


class Place:
    def __init__(self):
        self.tok = lax.axis_index("tok")
        self.col = lax.axis_index("col")
        self.z = self.tok // 2
        self.c = self.tok % 2
        self.x = self.col // NX
        self.y = self.col % NX
        self.sib = (self.zc(0, 1 - self.c), self.col)
        self.zn = ((self.zc(1, self.c), self.col), (self.zc(-1, self.c), self.col))

    def zc(self, dz, c):
        return ((self.z + dz + NZ) % NZ) * 2 + c

    def xy(self, dx, dy):
        return ((self.x + dx + NX) % NX) * NX + (self.y + dy + NX) % NX

    def peer(self, dx, dy):
        return (self.tok, self.xy(dx, dy))


def remote(src, dst, ssem, rsem, dev):
    return pltpu.make_async_remote_copy(
        src_ref=src, dst_ref=dst, send_sem=ssem, recv_sem=rsem, device_id=dev, device_id_type=MESH
    )


def greet(devices):
    barrier = pltpu.get_barrier_semaphore()
    for dev in devices:
        pl.semaphore_signal(barrier, inc=1, device_id=dev, device_id_type=MESH)
    pl.semaphore_wait(barrier, len(devices))


class Ring:
    def __init__(self, at, dst, rsend, rrecv, ssend, srecv, own):
        self.at, self.dst, self.own = at, dst, own
        self.ring, self.side = (rsend, rrecv), (ssend, srecv)
        self.sent = []

    def start(self, copy):
        copy.start()
        self.sent.append(copy)

    def block(self, d, h, s, core):
        return self.dst.at[pl.ds(self.at.zc(-s if d == 0 else s, core) * LOCAL + h * (LOCAL // 2), LOCAL // 2)]

    def hop(self, d, h, s):
        b = self.block(d, h, s, self.at.c)
        return remote(b, b, self.ring[0].at[d, h, s], self.ring[1].at[d, h, s], self.at.zn[d])

    def across(self, d, h, s, core):
        b = self.block(d, h, s, core)
        return remote(b, b, self.side[0].at[d, h, s - 1], self.side[1].at[d, h, s - 1], self.at.sib)

    def whole(self, core):
        b = self.dst.at[pl.ds(self.at.zc(0, core) * LOCAL, LOCAL)]
        return remote(b, b, self.own.at[0], self.own.at[1], self.at.sib)

    def begin(self):
        for h in range(2):
            for d in range(2):
                self.start(self.hop(d, h, 0))
        self.start(self.whole(self.at.c))

    def step(self, s, h):
        for d in range(2):
            if s > HOPS[d][h]:
                continue
            b = self.block(d, h, s, self.at.c)
            remote(b, b, self.ring[0].at[d, h, s - 1], self.ring[1].at[d, h, s - 1], self.at.zn[d]).wait_recv()
            if s < HOPS[d][h]:
                self.start(self.hop(d, h, s))
            self.start(self.across(d, h, s, self.at.c))

    def finish(self):
        other = 1 - self.at.c
        self.whole(other).wait_recv()
        for s in range(1, 9):
            for h in range(2):
                for d in range(2):
                    if s <= HOPS[d][h]:
                        self.across(d, h, s, other).wait_recv()

    def flush(self):
        for copy in self.sent:
            copy.wait_send()


def xy_gather(at, dst, n, cut, sends, recvs, first):
    sent = []
    lo, hi = pl.ds(0, cut), pl.ds(cut, n - cut)

    def shift(a, b):
        return (a, b) if first == 0 else (b, a)

    def dev(a, b):
        return at.peer(*shift(a, b))

    def slot(a, b):
        return dst.at[pl.ds(pl.multiple_of(at.xy(*shift(a, b)) * n, n), n)]

    def start(block, k, to):
        copy = remote(block, block, sends.at[k], recvs.at[k], to)
        copy.start()
        sent.append(copy)

    def wait(block, k, to):
        remote(block, block, sends.at[k], recvs.at[k], to).wait_recv()

    start(slot(0, 0), 0, dev(1, 0))
    start(slot(0, 0), 1, dev(-1, 0))
    start(slot(0, 0), 4, dev(0, 1))
    start(slot(0, 0), 5, dev(0, -1))
    yield
    wait(slot(-1, 0), 0, dev(1, 0))
    start(slot(-1, 0).at[lo], 2, dev(1, 0))
    wait(slot(1, 0), 1, dev(-1, 0))
    start(slot(1, 0).at[hi], 3, dev(-1, 0))
    for item, a in ((1, -1), (2, 1)):
        start(slot(a, 0), 4 + 4 * item, dev(0, 1))
        start(slot(a, 0), 5 + 4 * item, dev(0, -1))
    yield
    wait(slot(2, 0).at[lo], 2, dev(1, 0))
    wait(slot(2, 0).at[hi], 3, dev(-1, 0))
    start(slot(2, 0), 4 + 4 * 3, dev(0, 1))
    start(slot(2, 0), 5 + 4 * 3, dev(0, -1))
    yield
    for item, a in ((0, 0), (1, -1), (2, 1), (3, 2)):
        k = 4 + 4 * item
        wait(slot(a, -1), k, dev(0, 1))
        start(slot(a, -1).at[lo], k + 2, dev(0, 1))
        wait(slot(a, 1), k + 1, dev(0, -1))
        start(slot(a, 1).at[hi], k + 3, dev(0, -1))
        yield
    for item, a in ((0, 0), (1, -1), (2, 1), (3, 2)):
        k = 4 + 4 * item
        wait(slot(a, 2).at[lo], k + 2, dev(0, 1))
        wait(slot(a, 2).at[hi], k + 3, dev(0, -1))
    for copy in sent:
        copy.wait_send()


def xy_reduce(at, terms, n, first, waits, done, got1, part, got2, send1, recv1, send2, recv2):
    sent = []
    mine = (at.x, at.y) if first == 0 else (at.y, at.x)

    def dev(a, b):
        return at.peer(a, b) if first == 0 else at.peer(b, a)

    def line(i, size):
        return pl.ds(pl.multiple_of(((i + NX) % NX) * size, size), size)

    for k, a in enumerate((2, 1, -1)):
        copy = remote(terms.at[line(mine[0] + a, NX * n)], got1.at[k], send1.at[k], recv1.at[k], dev(a, 0))
        copy.start()
        sent.append(copy)
    for _ in range(waits[0]):
        yield
    for k, a in enumerate((2, 1, -1)):
        remote(got1.at[k], got1.at[k], send1.at[k], recv1.at[k], dev(a, 0)).wait_recv()

    def add(b, carry):
        v = terms[pl.ds(pl.multiple_of((mine[0] * NX + b) * n, n), n), :].astype(F32)
        rows = pl.ds(pl.multiple_of(b * n, n), n)
        for k in range(3):
            v = v + got1[k, rows, :].astype(F32)
        part[rows, :] = v.astype(part.dtype)
        return carry

    lax.fori_loop(0, NX, add, 0)
    for k, b in enumerate((2, 1, -1)):
        copy = remote(part.at[line(mine[1] + b, n)], got2.at[k], send2.at[k], recv2.at[k], dev(0, b))
        copy.start()
        sent.append(copy)
    for _ in range(waits[1]):
        yield
    for k, b in enumerate((2, 1, -1)):
        remote(got2.at[k], got2.at[k], send2.at[k], recv2.at[k], dev(0, b)).wait_recv()
    v = part[line(mine[1], n), :].astype(F32)
    for k in range(3):
        v = v + got2[k].astype(F32)
    done(v)
    for copy in sent:
        copy.wait_send()


def sub(h):
    return (0, 528, 176) if h == 0 else (528, 512, 128)


class RingSum:
    ORDER = (8, 7, -7, 6, -6, 5, -5, 4, -4, 3, -3, 2, -2, 1, -1, 0)

    def __init__(self, at, mine, theirs, stage, land, xsend, xrecv, rsend, rrecv):
        self.at, self.mine, self.theirs, self.stage, self.land = at, mine, theirs, stage, land
        self.side, self.ring = (xsend, xrecv), (rsend, rrecv)
        self.sent = []

    def give(self, off):
        copy = remote(
            self.mine.at[self.at.zc(off, 1 - self.at.c)],
            self.theirs.at[off + 7],
            self.side[0].at[off + 7],
            self.side[1].at[off + 7],
            self.at.sib,
        )
        copy.start()
        self.sent.append(copy)

    def wait_side(self, off):
        b = self.theirs.at[off + 7]
        remote(b, b, self.side[0].at[off + 7], self.side[1].at[off + 7], self.at.sib).wait_recv()

    def landed(self, d, h, s):
        first, size, tile = sub(h)
        b = self.land.at[d, s, pl.ds(first, size)]
        remote(b, b, self.ring[0].at[d, h, s], self.ring[1].at[d, h, s], self.at.zn[d]).wait_recv()

    def step(self, s, h):
        if h == 0:
            if s == 0:
                self.wait_side(8)
            if s < 7:
                self.wait_side(7 - s)
                self.wait_side(s - 7)
        first, size, tile = sub(h)
        for d in range(2):
            if s >= HOPS[d][h]:
                continue
            far = HOPS[d][h] - s
            off = far if d == 0 else -far
            buf = 8 if far == 8 else off
            owner = self.at.zc(off, self.at.c)
            if s:
                self.landed(d, h, s - 1)
            for t in range(size // tile):
                rows = pl.ds(first + t * tile, tile)
                v = self.mine[owner, rows, :].astype(F32) + self.theirs[buf + 7, rows, :].astype(F32)
                if s:
                    v = v + self.land[d, s - 1, rows, :].astype(F32)
                self.stage[d, s, rows, :] = v.astype(BF16)
            rows = pl.ds(first, size)
            copy = remote(
                self.stage.at[d, s, rows],
                self.land.at[d, s, rows],
                self.ring[0].at[d, h, s],
                self.ring[1].at[d, h, s],
                self.at.zn[d],
            )
            copy.start()
            self.sent.append(copy)

    def finish(self):
        self.wait_side(0)
        for h in range(2):
            for d in range(2):
                self.landed(d, h, HOPS[d][h] - 1)

    def total(self, rows, h):
        v = self.mine[self.at.tok, rows, :].astype(F32) + self.theirs[7, rows, :].astype(F32)
        for d in range(2):
            v = v + self.land[d, HOPS[d][h] - 1, rows, :].astype(F32)
        return v

    def flush(self):
        for copy in self.sent:
            copy.wait_send()


def dma(*shape):
    return pltpu.SemaphoreType.DMA(shape)


def vmem(dtype, *shape):
    return pltpu.VMEM(shape, dtype)


def by(gen, n):
    alive = True
    while alive:
        for _ in range(n):
            try:
                next(gen)
            except StopIteration:
                alive = False
                break
        if alive:
            yield


def joint(*gens):
    gens = list(gens)
    while gens:
        left = []
        for g in gens:
            try:
                next(g)
                left.append(g)
            except StopIteration:
                pass
        gens = left
        if gens:
            yield


RING_SEMS = [dma(2, 2, 8), dma(2, 2, 8), dma(2, 2, 8), dma(2, 2, 8), dma(2)]
RED_SEMS = [dma(3)] * 4

SCRATCH = dict(
    kbuf=[vmem(BF16, PAGES, PAGE, LANE)],
    vbuf=[vmem(BF16, PAGES, PAGE, LANE)],
    gbuf=[vmem(BF16, OWNERS, GROWS, LANE)],
    tbuf=[vmem(BF16, NCOL * HALF, LANE)] * 2,
    cbuf=[vmem(BF16, NCOL * HALF, LANE)] * 2,
    wqg=[vmem(BF16, KW, 2 * LANE)],
    qbuf=[vmem(BF16, ROWS, LANE)],
    act=[vmem(F32, ROWS, LANE)],
    grads=[vmem(BF16, NB, BLK, LANE)],
    gated=[vmem(BF16, ROWS, LANE)],
    scores=[vmem(F32, ROWS, 2 * LANE)] * 2,
    sums=[vmem(F32, SHARE, 2 * LANE)] * 2,
    wbuf=[vmem(BF16, ROWS, 2 * LANE)] * 2,
    wpick=[vmem(BF16, PAIRS, BLK, LANE)],
    sred_a=[vmem(F32, 3, NX * SHARE, 2 * LANE), vmem(F32, NX * SHARE, 2 * LANE), vmem(F32, 3, SHARE, 2 * LANE)] + RED_SEMS,
    sred_b=[vmem(F32, 3, NX * SHARE, 2 * LANE), vmem(F32, NX * SHARE, 2 * LANE), vmem(F32, 3, SHARE, 2 * LANE)] + RED_SEMS,
    ored_a=[vmem(BF16, 3, NX * HALF, LANE), vmem(BF16, NX * HALF, LANE), vmem(BF16, 3, HALF, LANE)] + RED_SEMS,
    ored_b=[vmem(BF16, 3, NX * HALF, LANE), vmem(BF16, NX * HALF, LANE), vmem(BF16, 3, HALF, LANE)] + RED_SEMS,
    gring=[
        vmem(BF16, NZ, GROWS, LANE),
        vmem(BF16, 2, 8, GROWS, LANE),
        vmem(BF16, 2, 8, GROWS, LANE),
        dma(16),
        dma(16),
        dma(2, 2, 8),
        dma(2, 2, 8),
    ],
    kring=RING_SEMS,
    vring=RING_SEMS,
    tsem=[dma(20)] * 4,
    csem=[dma(20)] * 4,
    wsem=[dma(20)] * 4,
)
NAMES = list(SCRATCH)
FLAT = [s for name in NAMES for s in SCRATCH[name]]


def kernel(pids, pair, block, mark, step_of, keys, tokens, cotangent, values, rate, wq, wg, wo, out, total, touched, *refs):
    refs = list(refs)
    s = {}
    for name in NAMES:
        n = len(SCRATCH[name])
        s[name], refs = refs[:n], refs[n:]
    (kbuf,), (vbuf,), (gbuf,), (wqg,), (qbuf,), (act,), (grads,), (gated,), (wpick,) = (
        s[n] for n in ("kbuf", "vbuf", "gbuf", "wqg", "qbuf", "act", "grads", "gated", "wpick")
    )
    at = Place()
    flags = set()
    greet([at.zn[0], at.zn[1], at.sib] + [at.peer(a, 0) for a in (1, -1, 2)] + [at.peer(0, a) for a in (1, -1, 2)])

    def factor(p):
        return jnp.exp(-(STEP - step_of[p]).astype(F32) * rate[...])

    kring = Ring(at, kbuf, *s["kring"])
    vring = Ring(at, vbuf, *s["vring"])
    gring = RingSum(at, gbuf, *s["gring"])

    def zchain():
        kbuf[pl.ds(at.tok * LOCAL, LOCAL)] = keys[...]
        kring.begin()
        for p in range(LOCAL):
            vbuf[at.tok * LOCAL + p] = (values[p] * factor(p)).astype(BF16)
        yield
        for step in range(1, 9):
            for h in range(2):
                kring.step(step, h)
                if (step, h) == (7, 1):
                    vring.begin()
                yield
        kring.finish()
        flags.add("keys")
        yield
        for step in range(1, 9):
            for h in range(2):
                vring.step(step, h)
                if step >= 7 and "grads" in flags and "begun" not in flags:
                    flags.add("begun")
                    gring.step(0, 0)
                    gring.step(0, 1)
                yield
        vring.finish()
        flags.add("values")
        while "grads" not in flags:
            yield
        if "begun" not in flags:
            gring.step(0, 0)
            gring.step(0, 1)
            yield
        for step in range(1, 8):
            for h in range(2):
                gring.step(step, h)
                yield
        gring.finish()

    def copy_in(src, bufs):
        rows = pl.ds(pl.multiple_of(at.col * HALF, HALF), HALF)
        for h in range(2):
            bufs[h][rows, :] = src[h * HALF : (h + 1) * HALF, :]

    def wide(buf, r):
        return jnp.concatenate(
            [buf[pl.ds(pl.multiple_of(k * HALF + r * 128, 128), 128), :] for k in range(NCOL)], axis=1
        )

    def forward():
        copy_in(tokens, s["tbuf"])
        copy_in(cotangent, s["cbuf"])
        gens = [xy_gather(at, s["tbuf"][f], HALF, 192, *s["tsem"][2 * f : 2 * f + 2], f) for f in range(2)]
        yield from joint(*gens)
        flags.add("tokens")
        wqg[:, :LANE] = wq[...]
        wqg[:, LANE:] = wg[...]
        for h in range(2):

            def tile(r, carry, h=h):
                both = jnp.dot(wide(s["tbuf"][h], r), wqg[...], preferred_element_type=F32)
                rows = pl.ds(pl.multiple_of(h * HALF + r * 128, 128), 128)
                qbuf[rows, :] = both[:, :LANE].astype(BF16)
                g = both[:, LANE:]
                act[rows, :] = g / (1.0 + jnp.exp(-g))
                return carry

            lax.fori_loop(0, 3, tile, 0)
            yield
        flags.add("queries")

    def backward():
        for _ in range(6):
            yield
        gens = [xy_gather(at, s["cbuf"][f], HALF, 192, *s["csem"][2 * f : 2 * f + 2], f) for f in range(2)]
        yield from joint(*gens)
        while "queries" not in flags:
            yield
        for h in range(2):

            def tile(r, carry, h=h):
                g = lax.dot_general(
                    wide(s["cbuf"][h], r), wo[...], (((1,), (1,)), ((), ())), preferred_element_type=F32
                )
                rows = pl.ds(pl.multiple_of(h * HALF + r * 128, 128), 128)
                g = (g * act[rows, :]).astype(BF16)
                grads[h * (NB // 2) + 2 * r] = g[:BLK]
                grads[h * (NB // 2) + 2 * r + 1] = g[BLK:]
                return carry

            lax.fori_loop(0, 3, tile, 0)
            yield
        flags.add("backward")

    def lookup():
        while not {"keys", "queries"} <= flags:
            yield
        for b in range(NB):
            q = qbuf[b * BLK : (b + 1) * BLK, :]
            for i in range(PICKS):
                page = kbuf[pids[b * PICKS + i]]
                v = lax.dot_general(q, page, (((1,), (1,)), ((), ())), preferred_element_type=F32)
                lanes = slice((i % 2) * PAGE, (i % 2 + 1) * PAGE)
                r = 0
                while r < BLK:
                    row = b * BLK + r
                    j, o = row // SHARE, row % SHARE
                    size = min(SHARE - o, BLK - r)
                    spot = j if i < 2 else (j % NX) * NX + j // NX
                    s["scores"][i // 2][spot * SHARE + o : spot * SHARE + o + size, lanes] = v[r : r + size]
                    r += size
            if b % 6 == 5:
                yield

        def keep(f):
            def done(v):
                s["sums"][f][...] = v * (KW**-0.5)

            return done

        gens = [
            xy_reduce(at, s["scores"][f], SHARE, f, (3, 1), keep(f), *s["sred_b" if f else "sred_a"]) for f in range(2)
        ]
        yield from joint(*gens)
        left, right = s["sums"][0][...], s["sums"][1][...]
        top = jnp.maximum(jnp.max(left, axis=1, keepdims=True), jnp.max(right, axis=1, keepdims=True))
        left, right = jnp.exp(left - top), jnp.exp(right - top)
        total = jnp.sum(left, axis=1, keepdims=True) + jnp.sum(right, axis=1, keepdims=True)
        rows = pl.ds(pl.multiple_of(at.col * SHARE, SHARE), SHARE)
        s["wbuf"][0][rows, :] = (left / total).astype(BF16)
        s["wbuf"][1][rows, :] = (right / total).astype(BF16)
        gens = [xy_gather(at, s["wbuf"][f], SHARE, 16 + 16 * f, *s["wsem"][2 * f : 2 * f + 2], f) for f in range(2)]
        yield from by(joint(*gens), 3)
        for b in range(NB):
            for i in range(PICKS):
                lanes = slice((i % 2) * PAGE, (i % 2 + 1) * PAGE)
                wpick[b * PICKS + i] = s["wbuf"][i // 2][b * BLK : (b + 1) * BLK, lanes]
        flags.add("weights")
        while "backward" not in flags:
            yield
        for off in RingSum.ORDER:
            for core in range(2):
                owner = at.zc(off, core)
                found = []
                for k in range(2):
                    n = owner * 2 + k
                    v = lax.dot_general(
                        wpick[pair[n]], grads[block[n]], (((0,), (0,)), ((), ())), preferred_element_type=F32
                    )
                    found.append((v, [mark[n * LOCAL + p] for p in range(LOCAL)]))
                row = lax.broadcasted_iota(jnp.int32, (CNT, LANE), 0)
                count = jnp.zeros((CNT, LANE), F32)
                for p in range(LOCAL):
                    v = found[0][0] * found[0][1][p] + found[1][0] * found[1][1][p]
                    gbuf[owner, p * PAGE : (p + 1) * PAGE, :] = v.astype(BF16)
                    count = jnp.where(row == p, found[0][1][p] + found[1][1][p], count)
                gbuf[owner, OWN:, :] = count.astype(BF16)
            gring.give(off)
            if off in (-7, -5, -3, -1):
                yield
        flags.add("grads")
        yield
        while "values" not in flags:
            yield

        def mix(b, carry):
            rows = pl.ds(pl.multiple_of(b * BLK, BLK), BLK)
            m = jnp.zeros((BLK, LANE), F32)
            for i in range(PICKS):
                n = b * PICKS + i
                m += jnp.dot(wpick[n], vbuf[pids[n]], preferred_element_type=F32)
            gated[rows, :] = (m * act[rows, :]).astype(BF16)
            return carry

        lax.fori_loop(0, NB, mix, 0)
        yield
        for k in range(NCOL):
            o = jnp.dot(gated[...], wo[:, k * LANE : (k + 1) * LANE], preferred_element_type=F32).astype(BF16)
            turned = (k % NX) * NX + k // NX
            s["tbuf"][0][k * HALF : (k + 1) * HALF, :] = o[:HALF]
            s["tbuf"][1][turned * HALF : (turned + 1) * HALF, :] = o[HALF:]
            if k % 8 == 7:
                yield

        def give(f):
            def done(v):
                out[f * HALF : (f + 1) * HALF, :] = v.astype(BF16)

            return done

        gens = [xy_reduce(at, s["tbuf"][f], HALF, f, (7, 2), give(f), *s["ored_b" if f else "ored_a"]) for f in range(2)]
        yield from joint(*gens)

    for _ in joint(zchain(), forward(), backward(), lookup()):
        pass
    touched[...] = gring.total(pl.ds(OWN, CNT), 1)
    for h, lo, hi in ((0, 0, 528), (1, 528, OWN)):
        for a in range(lo, hi, 16):
            rows = pl.ds(a, 16)
            total[rows, :] = gring.total(rows, h)
    kring.flush()
    vring.flush()
    gring.flush()


def settle_kernel(step_of, rate, raw, total, touched, values, momentum, out, new_values, new_momentum):
    out[...] = raw[...]
    for p in range(LOCAL):
        f = jnp.exp(-(STEP - step_of[p]).astype(F32) * rate[...])
        hit = touched[p : p + 1, :] > 0.5
        v, m = values[p], momentum[p]
        m = jnp.where(hit, MOMENTUM_RATE * m + total[p] * f, m)
        new_momentum[p] = m
        new_values[p] = jnp.where(hit, v * f - LEARN_RATE * m, v)


def per_device(
    tokens,
    cotangent,
    query_weight,
    slot_keys,
    values,
    momentum,
    page_ids,
    last_step,
    decay_rate,
    gate_weight,
    out_weight,
):
    pids = page_ids.reshape(-1)
    match = (pids // LOCAL)[None, :] == jnp.arange(OWNERS)[:, None]
    code = (jnp.arange(PAIRS) * LOCAL + pids % LOCAL)[None, :]
    none = PAIRS * LOCAL
    first = jnp.min(jnp.where(match, code, none), axis=1)
    last = jnp.max(jnp.where(match, code, -1), axis=1)
    both = jnp.stack([first, last], axis=1)
    valid = jnp.stack([first < none, last > first], axis=1)
    both = jnp.where(valid, both, 0)
    pair = (both // LOCAL).reshape(-1)
    mark = (valid[:, :, None] & ((both % LOCAL)[:, :, None] == jnp.arange(LOCAL))).astype(F32).reshape(-1)
    paged = (LOCAL, PAGE, LANE)
    rate = decay_rate.reshape(1, LANE)
    stored = values.reshape(paged)
    raw, total, touched = pl.pallas_call(
        kernel,
        out_shape=(
            jax.ShapeDtypeStruct((ROWS, LANE), BF16),
            jax.ShapeDtypeStruct((OWN, LANE), F32),
            jax.ShapeDtypeStruct((CNT, LANE), F32),
        ),
        in_specs=[SM] * 5 + [VM] * 8,
        out_specs=(VM,) * 3,
        scratch_shapes=FLAT,
        compiler_params=pltpu.CompilerParams(collective_id=0, has_side_effects=True, vmem_limit_bytes=60 << 20),
    )(
        pids,
        pair,
        pair // PICKS,
        mark,
        last_step,
        slot_keys.reshape(paged),
        tokens,
        cotangent,
        stored,
        rate,
        query_weight,
        gate_weight,
        out_weight,
    )
    layer_out, new_values, new_momentum = pl.pallas_call(
        settle_kernel,
        out_shape=(
            jax.ShapeDtypeStruct((ROWS, LANE), BF16),
            jax.ShapeDtypeStruct(paged, F32),
            jax.ShapeDtypeStruct(paged, F32),
        ),
        in_specs=[SM] + [VM] * 6,
        out_specs=(VM,) * 3,
    )(last_step, rate, raw, total.reshape(paged), touched, stored, momentum.reshape(paged))
    return (layer_out, new_values.reshape(OWN, LANE), new_momentum.reshape(OWN, LANE))


def solution(mesh):
    in_specs = (
        P("tok", "col"),
        P("tok", "col"),
        P(None, "col"),
        P("tok", "col"),
        P("tok", "col"),
        P("tok", "col"),
        P("tok", None),
        P("tok"),
        P("col"),
        P(None, "col"),
        P("col", None),
    )
    out_specs = (P("tok", "col"), P("tok", "col"), P("tok", "col"))
    return jax.shard_map(
        per_device, mesh=mesh, in_specs=in_specs, out_specs=out_specs, check_vma=False
    )
```

```python
import jax
import jax.numpy as jnp
from jax import lax
from jax.experimental import pallas as pl
from jax.experimental.pallas import tpu as pltpu
from jax.sharding import PartitionSpec as P

KW = 2048
STEP = 64
MOMENTUM_RATE = 0.9
LEARN_RATE = 1.0

NZ = 16
NX = 4
NCOL = 16
ROWS = 768
NB = 12
PICKS = 4
PAIRS = NB * PICKS
BLK = 64
PAGE = 128
LANE = 128
LOCAL = 8
OWNERS = 2 * NZ
PAGES = OWNERS * LOCAL
OWN = 1024
SHARE = ROWS // NCOL
HALF = ROWS // 2
CNT = 16
GROWS = OWN + CNT
TSTART = 3
TPACE = ()
CSTART = 8
CPACE = (3,)
MESH = pl.DeviceIdType.MESH
HOPS = ((8, 7), (7, 8))
VM = pl.BlockSpec(memory_space=pltpu.VMEM)
ANY = pl.BlockSpec(memory_space=pl.ANY)
SM = pl.BlockSpec(memory_space=pltpu.SMEM)
F32 = jnp.float32
BF16 = jnp.bfloat16


class Place:
    def __init__(self):
        self.tok = lax.axis_index("tok")
        self.col = lax.axis_index("col")
        self.z = self.tok // 2
        self.c = self.tok % 2
        self.x = self.col // NX
        self.y = self.col % NX
        self.sib = (self.zc(0, 1 - self.c), self.col)
        self.zn = ((self.zc(1, self.c), self.col), (self.zc(-1, self.c), self.col))

    def zc(self, dz, c):
        return ((self.z + dz + NZ) % NZ) * 2 + c

    def xy(self, dx, dy):
        return ((self.x + dx + NX) % NX) * NX + (self.y + dy + NX) % NX

    def peer(self, dx, dy):
        return (self.tok, self.xy(dx, dy))


def remote(src, dst, ssem, rsem, dev):
    return pltpu.make_async_remote_copy(
        src_ref=src, dst_ref=dst, send_sem=ssem, recv_sem=rsem, device_id=dev, device_id_type=MESH
    )


def greet(devices):
    barrier = pltpu.get_barrier_semaphore()
    for dev in devices:
        pl.semaphore_signal(barrier, inc=1, device_id=dev, device_id_type=MESH)
    pl.semaphore_wait(barrier, len(devices))


class Ring:
    def __init__(self, at, src, dst, rsend, rrecv, ssend, srecv, own):
        self.at, self.src, self.dst, self.own = at, src, dst, own
        self.ring, self.side = (rsend, rrecv), (ssend, srecv)
        self.sent = []

    def start(self, copy):
        copy.start()
        self.sent.append(copy)

    def block(self, d, h, s, core):
        return self.dst.at[pl.ds(self.at.zc(-s if d == 0 else s, core) * LOCAL + h * (LOCAL // 2), LOCAL // 2)]

    def hop(self, d, h, s):
        b = self.block(d, h, s, self.at.c)
        from_ = b if s else self.src.at[pl.ds(h * (LOCAL // 2), LOCAL // 2)]
        return remote(from_, b, self.ring[0].at[d, h, s], self.ring[1].at[d, h, s], self.at.zn[d])

    def across(self, d, h, s, core):
        b = self.block(d, h, s, core)
        return remote(b, b, self.side[0].at[d, h, s - 1], self.side[1].at[d, h, s - 1], self.at.sib)

    def whole(self):
        b = self.dst.at[pl.ds(self.at.zc(0, 1 - self.at.c) * LOCAL, LOCAL)]
        return remote(b, b, self.own.at[0], self.own.at[1], self.at.sib)

    def begin(self):
        for h in range(2):
            for d in range(2):
                self.start(self.hop(d, h, 0))
        b = self.dst.at[pl.ds(self.at.tok * LOCAL, LOCAL)]
        self.start(remote(self.src, b, self.own.at[0], self.own.at[1], self.at.sib))

    def step(self, s, h):
        for d in range(2):
            if s > HOPS[d][h]:
                continue
            b = self.block(d, h, s, self.at.c)
            remote(b, b, self.ring[0].at[d, h, s - 1], self.ring[1].at[d, h, s - 1], self.at.zn[d]).wait_recv()
            if s < HOPS[d][h]:
                self.start(self.hop(d, h, s))
            self.start(self.across(d, h, s, self.at.c))

    def finish(self):
        other = 1 - self.at.c
        self.whole().wait_recv()
        for s in range(1, 9):
            for h in range(2):
                for d in range(2):
                    if s <= HOPS[d][h]:
                        self.across(d, h, s, other).wait_recv()

    def flush(self):
        for copy in self.sent:
            copy.wait_send()


def xy_gather(at, src, dst, n, cut, sends, recvs, first):
    sent = []
    lo, hi = pl.ds(0, cut), pl.ds(cut, n - cut)

    def shift(a, b):
        return (a, b) if first == 0 else (b, a)

    def dev(a, b):
        return at.peer(*shift(a, b))

    def slot(a, b):
        return dst.at[pl.ds(pl.multiple_of(at.xy(*shift(a, b)) * n, n), n)]

    def start(block, k, to):
        copy = remote(block, block, sends.at[k], recvs.at[k], to)
        copy.start()
        sent.append(copy)

    def wait(block, k, to):
        remote(block, block, sends.at[k], recvs.at[k], to).wait_recv()

    for k, to in ((0, dev(1, 0)), (1, dev(-1, 0)), (4, dev(0, 1)), (5, dev(0, -1))):
        copy = remote(src, slot(0, 0), sends.at[k], recvs.at[k], to)
        copy.start()
        sent.append(copy)
    yield
    wait(slot(-1, 0), 0, dev(1, 0))
    start(slot(-1, 0).at[lo], 2, dev(1, 0))
    wait(slot(1, 0), 1, dev(-1, 0))
    start(slot(1, 0).at[hi], 3, dev(-1, 0))
    for item, a in ((1, -1), (2, 1)):
        start(slot(a, 0), 4 + 4 * item, dev(0, 1))
        start(slot(a, 0), 5 + 4 * item, dev(0, -1))
    yield
    wait(slot(2, 0).at[lo], 2, dev(1, 0))
    wait(slot(2, 0).at[hi], 3, dev(-1, 0))
    start(slot(2, 0), 4 + 4 * 3, dev(0, 1))
    start(slot(2, 0), 5 + 4 * 3, dev(0, -1))
    yield
    for item, a in ((0, 0), (1, -1), (2, 1), (3, 2)):
        k = 4 + 4 * item
        wait(slot(a, -1), k, dev(0, 1))
        start(slot(a, -1).at[lo], k + 2, dev(0, 1))
        wait(slot(a, 1), k + 1, dev(0, -1))
        start(slot(a, 1).at[hi], k + 3, dev(0, -1))
        yield
    for item, a in ((0, 0), (1, -1), (2, 1), (3, 2)):
        k = 4 + 4 * item
        wait(slot(a, 2).at[lo], k + 2, dev(0, 1))
        wait(slot(a, 2).at[hi], k + 3, dev(0, -1))
    for copy in sent:
        copy.wait_send()


def xy_spread(at, dst, n, sends, recvs, first, waits):
    sent = []

    def dev(a, b):
        return at.peer(a, b) if first == 0 else at.peer(b, a)

    def slot(a, b):
        i = at.xy(a, b) if first == 0 else at.xy(b, a)
        return dst.at[pl.ds(pl.multiple_of(i * n, n), n)]

    def start(block, k, to):
        copy = remote(block, block, sends.at[k], recvs.at[k], to)
        copy.start()
        sent.append(copy)

    def wait(block, k, to):
        remote(block, block, sends.at[k], recvs.at[k], to).wait_recv()

    line = (2, 1, -1)
    for k, a in enumerate(line):
        start(slot(0, 0), k, dev(a, 0))
    for k, b in enumerate(line):
        start(slot(0, 0), 3 + k, dev(0, b))
    for _ in range(waits[0]):
        yield
    for j, a in enumerate(line):
        wait(slot(-a, 0), j, dev(a, 0))
        for k, b in enumerate(line):
            start(slot(-a, 0), 6 + 3 * j + k, dev(0, b))
    for _ in range(waits[1]):
        yield
    for k, b in enumerate(line):
        wait(slot(0, -b), 3 + k, dev(0, b))
        for j, a in enumerate(line):
            wait(slot(-a, -b), 6 + 3 * j + k, dev(0, b))
    for copy in sent:
        copy.wait_send()


def xy_reduce(at, terms, n, first, waits, done, got1, part, got2, send1, recv1, send2, recv2):
    sent = []
    mine = (at.x, at.y) if first == 0 else (at.y, at.x)

    def dev(a, b):
        return at.peer(a, b) if first == 0 else at.peer(b, a)

    def line(i, size):
        return pl.ds(pl.multiple_of(((i + NX) % NX) * size, size), size)

    for k, a in enumerate((2, 1, -1)):
        copy = remote(terms.at[line(mine[0] + a, NX * n)], got1.at[k], send1.at[k], recv1.at[k], dev(a, 0))
        copy.start()
        sent.append(copy)
    for _ in range(waits[0]):
        yield
    for k, a in enumerate((2, 1, -1)):
        remote(got1.at[k], got1.at[k], send1.at[k], recv1.at[k], dev(a, 0)).wait_recv()

    def add(b, carry):
        v = terms[pl.ds(pl.multiple_of((mine[0] * NX + b) * n, n), n), :].astype(F32)
        rows = pl.ds(pl.multiple_of(b * n, n), n)
        for k in range(3):
            v = v + got1[k, rows, :].astype(F32)
        part[rows, :] = v.astype(part.dtype)
        return carry

    lax.fori_loop(0, NX, add, 0)
    for k, b in enumerate((2, 1, -1)):
        copy = remote(part.at[line(mine[1] + b, n)], got2.at[k], send2.at[k], recv2.at[k], dev(0, b))
        copy.start()
        sent.append(copy)
    for _ in range(waits[1]):
        yield
    for k, b in enumerate((2, 1, -1)):
        remote(got2.at[k], got2.at[k], send2.at[k], recv2.at[k], dev(0, b)).wait_recv()
    v = part[line(mine[1], n), :].astype(F32)
    for k in range(3):
        v = v + got2[k].astype(F32)
    done(v)
    for copy in sent:
        copy.wait_send()


def sub(h):
    return (0, 528, 176) if h == 0 else (528, 512, 128)


class RingSum:
    ORDER = (8, 7, -7, 6, -6, 5, -5, 4, -4, 3, -3, 2, -2, 1, -1, 0)

    def __init__(self, at, mine, theirs, stage, land, xsend, xrecv, rsend, rrecv):
        self.at, self.mine, self.theirs, self.stage, self.land = at, mine, theirs, stage, land
        self.side, self.ring = (xsend, xrecv), (rsend, rrecv)
        self.sent = []

    def give(self, off):
        copy = remote(
            self.mine.at[self.at.zc(off, 1 - self.at.c)],
            self.theirs.at[off + 7],
            self.side[0].at[off + 7],
            self.side[1].at[off + 7],
            self.at.sib,
        )
        copy.start()
        self.sent.append(copy)

    def wait_side(self, off):
        b = self.theirs.at[off + 7]
        remote(b, b, self.side[0].at[off + 7], self.side[1].at[off + 7], self.at.sib).wait_recv()

    def landed(self, d, h, s):
        first, size, tile = sub(h)
        b = self.land.at[d, s, pl.ds(first, size)]
        remote(b, b, self.ring[0].at[d, h, s], self.ring[1].at[d, h, s], self.at.zn[d]).wait_recv()

    def step(self, s, h):
        if h == 0:
            if s == 0:
                self.wait_side(8)
            if s < 7:
                self.wait_side(7 - s)
                self.wait_side(s - 7)
        first, size, tile = sub(h)
        for d in range(2):
            if s >= HOPS[d][h]:
                continue
            far = HOPS[d][h] - s
            off = far if d == 0 else -far
            buf = 8 if far == 8 else off
            owner = self.at.zc(off, self.at.c)
            if s:
                self.landed(d, h, s - 1)
            for t in range(size // tile):
                rows = pl.ds(first + t * tile, tile)
                v = self.mine[owner, rows, :].astype(F32) + self.theirs[buf + 7, rows, :].astype(F32)
                if s:
                    v = v + self.land[d, s - 1, rows, :].astype(F32)
                self.stage[d, s, rows, :] = v.astype(BF16)
            rows = pl.ds(first, size)
            copy = remote(
                self.stage.at[d, s, rows],
                self.land.at[d, s, rows],
                self.ring[0].at[d, h, s],
                self.ring[1].at[d, h, s],
                self.at.zn[d],
            )
            copy.start()
            self.sent.append(copy)

    def finish(self):
        self.wait_side(0)
        for h in range(2):
            for d in range(2):
                self.landed(d, h, HOPS[d][h] - 1)

    def total(self, rows, h):
        v = self.mine[self.at.tok, rows, :].astype(F32) + self.theirs[7, rows, :].astype(F32)
        for d in range(2):
            v = v + self.land[d, HOPS[d][h] - 1, rows, :].astype(F32)
        return v

    def flush(self):
        for copy in self.sent:
            copy.wait_send()


def dma(*shape):
    return pltpu.SemaphoreType.DMA(shape)


def vmem(dtype, *shape):
    return pltpu.VMEM(shape, dtype)


def paced(gen, waits):
    for i, _ in enumerate(gen):
        for _ in range(waits[i] if i < len(waits) else 1):
            yield


def joint(*gens):
    gens = list(gens)
    while gens:
        left = []
        for g in gens:
            try:
                next(g)
                left.append(g)
            except StopIteration:
                pass
        gens = left
        if gens:
            yield


RING_SEMS = [dma(2, 2, 8), dma(2, 2, 8), dma(2, 2, 8), dma(2, 2, 8), dma(2)]
RED_SEMS = [dma(3)] * 4

SCRATCH = dict(
    kbuf=[vmem(BF16, PAGES, PAGE, LANE)],
    vbuf=[vmem(BF16, PAGES, PAGE, LANE)],
    gbuf=[vmem(BF16, OWNERS, GROWS, LANE)],
    tbuf=[vmem(BF16, NCOL * HALF, LANE)] * 2,
    cbuf=[vmem(BF16, NCOL * HALF, LANE)] * 2,
    wqg=[vmem(BF16, KW, 2 * LANE)],
    wobuf=[vmem(BF16, LANE, KW)],
    wot=[vmem(BF16, KW, LANE)],
    stored=[vmem(F32, LOCAL, PAGE, LANE)],
    local=[dma(10)],
    qbuf=[vmem(BF16, ROWS, LANE)],
    act=[vmem(F32, ROWS, LANE)],
    grads=[vmem(BF16, NB, BLK, LANE)],
    gated=[vmem(BF16, ROWS, LANE)],
    scores=[vmem(F32, ROWS, 2 * LANE)] * 2,
    sums=[vmem(F32, SHARE, 2 * LANE)] * 2,
    wbuf=[vmem(BF16, ROWS, 2 * LANE)] * 2,
    wpick=[vmem(BF16, PAIRS, BLK, LANE)],
    sred_a=[vmem(F32, 3, NX * SHARE, 2 * LANE), vmem(F32, NX * SHARE, 2 * LANE), vmem(F32, 3, SHARE, 2 * LANE)] + RED_SEMS,
    sred_b=[vmem(F32, 3, NX * SHARE, 2 * LANE), vmem(F32, NX * SHARE, 2 * LANE), vmem(F32, 3, SHARE, 2 * LANE)] + RED_SEMS,
    ored_a=[vmem(BF16, 3, NX * HALF, LANE), vmem(BF16, NX * HALF, LANE), vmem(BF16, 3, HALF, LANE)] + RED_SEMS,
    ored_b=[vmem(BF16, 3, NX * HALF, LANE), vmem(BF16, NX * HALF, LANE), vmem(BF16, 3, HALF, LANE)] + RED_SEMS,
    gring=[
        vmem(BF16, NZ, GROWS, LANE),
        vmem(BF16, 2, 8, GROWS, LANE),
        vmem(BF16, 2, 8, GROWS, LANE),
        dma(16),
        dma(16),
        dma(2, 2, 8),
        dma(2, 2, 8),
    ],
    kring=RING_SEMS,
    vring=RING_SEMS,
    tsem=[dma(20)] * 4,
    csem=[dma(20)] * 4,
    wsem=[dma(15)] * 4,
)
NAMES = list(SCRATCH)
FLAT = [s for name in NAMES for s in SCRATCH[name]]


def kernel(pids, pair, block, mark, step_of, keys, tokens, cotangent, values, rate, wq, wg, wo, out, total, touched, *refs):
    refs = list(refs)
    s = {}
    for name in NAMES:
        n = len(SCRATCH[name])
        s[name], refs = refs[:n], refs[n:]
    (kbuf,), (vbuf,), (gbuf,), (wqg,), (qbuf,), (act,), (grads,), (gated,), (wpick,), (local,) = (
        s[n] for n in ("kbuf", "vbuf", "gbuf", "wqg", "qbuf", "act", "grads", "gated", "wpick", "local")
    )
    (wobuf,), (wot,), (stored,) = s["wobuf"], s["wot"], s["stored"]
    at = Place()
    flags = set()
    greet([at.zn[0], at.zn[1], at.sib] + [at.peer(a, 0) for a in (1, -1, 2)] + [at.peer(0, a) for a in (1, -1, 2)])

    def factor(p):
        return jnp.exp(-(STEP - step_of[p]).astype(F32) * rate[...])

    mine = pl.ds(at.tok * LOCAL, LOCAL)
    kring = Ring(at, keys, kbuf, *s["kring"])
    vring = Ring(at, vbuf.at[mine], vbuf, *s["vring"])
    places = pl.ds(pl.multiple_of(at.col * HALF, HALF), HALF)

    def fetch(k, src, dst):
        copy = pltpu.make_async_copy(src, dst, local.at[k])
        copy.start()
        return copy

    halves = (pl.ds(0, HALF), pl.ds(HALF, HALF))
    gring = RingSum(at, gbuf, *s["gring"])

    def zchain():
        kring.begin()
        yield
        got = fetch(0, keys, kbuf.at[mine]), fetch(1, values, stored)
        yield
        for step in range(1, 9):
            for h in range(2):
                kring.step(step, h)
                if (step, h) == (7, 1):
                    vring.begin()
                yield
                if (step, h) == (2, 0):
                    for copy in got:
                        copy.wait()
                    for p in range(LOCAL):
                        vbuf[at.tok * LOCAL + p] = (stored[p] * factor(p)).astype(BF16)
        kring.finish()
        flags.add("keys")
        yield
        for step in range(1, 9):
            for h in range(2):
                vring.step(step, h)
                if step >= 7 and 7 in flags and "begun" not in flags:
                    flags.add("begun")
                    gring.step(0, 0)
                    gring.step(0, 1)
                yield
        vring.finish()
        flags.add("values")
        while 7 not in flags:
            yield
        if "begun" not in flags:
            gring.step(0, 0)
            gring.step(0, 1)
            yield
        for step in range(1, 8):
            while 7 - step not in flags:
                yield
            for h in range(2):
                gring.step(step, h)
                yield
        gring.finish()

    def wide(buf, r):
        return jnp.concatenate(
            [buf[pl.ds(pl.multiple_of(k * HALF + r * 128, 128), 128), :] for k in range(NCOL)], axis=1
        )

    def forward():
        gens = [
            xy_gather(at, tokens.at[halves[f]], s["tbuf"][f], HALF, 192, *s["tsem"][2 * f : 2 * f + 2], f) for f in range(2)
        ]
        gathered = joint(*gens)
        next(gathered)
        got = [fetch(2 + f, tokens.at[halves[f]], s["tbuf"][f].at[places]) for f in range(2)]
        got.append(fetch(4, wq, wqg.at[:, pl.ds(0, LANE)]))
        got.append(fetch(5, wg, wqg.at[:, pl.ds(LANE, LANE)]))
        got.append(fetch(6, wo, wobuf))
        got += [fetch(7 + f, cotangent.at[halves[f]], s["cbuf"][f].at[places]) for f in range(2)]
        for _ in range(TSTART):
            yield
        yield from paced(gathered, TPACE)
        for copy in got:
            copy.wait()
        flags.add("tokens")
        for h in range(2):

            def tile(r, carry, h=h):
                both = jnp.dot(wide(s["tbuf"][h], r), wqg[...], preferred_element_type=F32)
                rows = pl.ds(pl.multiple_of(h * HALF + r * 128, 128), 128)
                qbuf[rows, :] = both[:, :LANE].astype(BF16)
                g = both[:, LANE:]
                act[rows, :] = g / (1.0 + jnp.exp(-g))
                return carry

            for r in range(3):
                lax.fori_loop(r, r + 1, tile, 0)
                yield
        wot[...] = wobuf[...].T
        yield
        flags.add("queries")

    def backward():
        for _ in range(CSTART):
            yield
        gens = [xy_gather(at, cotangent.at[halves[f]], s["cbuf"][f], HALF, 192, *s["csem"][2 * f : 2 * f + 2], f) for f in range(2)]
        yield from paced(joint(*gens), CPACE)
        while "queries" not in flags:
            yield
        for h in range(2):

            def tile(r, carry, h=h):
                g = jnp.dot(wide(s["cbuf"][h], r), wot[...], preferred_element_type=F32)
                rows = pl.ds(pl.multiple_of(h * HALF + r * 128, 128), 128)
                g = (g * act[rows, :]).astype(BF16)
                grads[h * (NB // 2) + 2 * r] = g[:BLK]
                grads[h * (NB // 2) + 2 * r + 1] = g[BLK:]
                return carry

            for lo, hi in ((0, 2), (2, 3)):
                lax.fori_loop(lo, hi, tile, 0)
                yield
        flags.add("backward")

    def lookup():
        while not {"keys", "queries"} <= flags:
            yield
        for b in range(NB):
            q = qbuf[b * BLK : (b + 1) * BLK, :]
            for i in range(PICKS):
                page = kbuf[pids[b * PICKS + i]]
                v = lax.dot_general(q, page, (((1,), (1,)), ((), ())), preferred_element_type=F32)
                lanes = slice((i % 2) * PAGE, (i % 2 + 1) * PAGE)
                r = 0
                while r < BLK:
                    row = b * BLK + r
                    j, o = row // SHARE, row % SHARE
                    size = min(SHARE - o, BLK - r)
                    spot = j if i < 2 else (j % NX) * NX + j // NX
                    s["scores"][i // 2][spot * SHARE + o : spot * SHARE + o + size, lanes] = v[r : r + size]
                    r += size
            if b % 6 == 5:
                yield

        def keep(f):
            def done(v):
                s["sums"][f][...] = v * (KW**-0.5)

            return done

        gens = [
            xy_reduce(at, s["scores"][f], SHARE, f, (3, 1), keep(f), *s["sred_b" if f else "sred_a"]) for f in range(2)
        ]
        yield from joint(*gens)
        left, right = s["sums"][0][...], s["sums"][1][...]
        top = jnp.maximum(jnp.max(left, axis=1, keepdims=True), jnp.max(right, axis=1, keepdims=True))
        left, right = jnp.exp(left - top), jnp.exp(right - top)
        total = jnp.sum(left, axis=1, keepdims=True) + jnp.sum(right, axis=1, keepdims=True)
        rows = pl.ds(pl.multiple_of(at.col * SHARE, SHARE), SHARE)
        s["wbuf"][0][rows, :] = (left / total).astype(BF16)
        s["wbuf"][1][rows, :] = (right / total).astype(BF16)
        gens = [xy_spread(at, s["wbuf"][f], SHARE, *s["wsem"][2 * f : 2 * f + 2], f, (2, 2)) for f in range(2)]
        yield from joint(*gens)
        for b in range(NB):
            for i in range(PICKS):
                lanes = slice((i % 2) * PAGE, (i % 2 + 1) * PAGE)
                wpick[b * PICKS + i] = s["wbuf"][i // 2][b * BLK : (b + 1) * BLK, lanes]
        flags.add("weights")
        while "backward" not in flags:
            yield
        for off in RingSum.ORDER:
            for core in range(2):
                owner = at.zc(off, core)
                found = []
                for k in range(2):
                    n = owner * 2 + k
                    v = lax.dot_general(
                        wpick[pair[n]], grads[block[n]], (((0,), (0,)), ((), ())), preferred_element_type=F32
                    )
                    found.append((v, [mark[n * LOCAL + p] for p in range(LOCAL)]))
                row = lax.broadcasted_iota(jnp.int32, (CNT, LANE), 0)
                count = jnp.zeros((CNT, LANE), F32)
                for p in range(LOCAL):
                    v = found[0][0] * found[0][1][p] + found[1][0] * found[1][1][p]
                    gbuf[owner, p * PAGE : (p + 1) * PAGE, :] = v.astype(BF16)
                    count = jnp.where(row == p, found[0][1][p] + found[1][1][p], count)
                gbuf[owner, OWN:, :] = count.astype(BF16)
            gring.give(off)
            if off <= 0:
                flags.add(-off)
                if off in (-7, -5, -3, -1, 0):
                    yield
        while "values" not in flags:
            yield

        def mix(b, carry):
            rows = pl.ds(pl.multiple_of(b * BLK, BLK), BLK)
            m = jnp.zeros((BLK, LANE), F32)
            for i in range(PICKS):
                n = b * PICKS + i
                m += jnp.dot(wpick[n], vbuf[pids[n]], preferred_element_type=F32)
            gated[rows, :] = (m * act[rows, :]).astype(BF16)
            return carry

        for b in (0, 6):
            lax.fori_loop(b, b + 6, mix, 0)
            yield
        for k in range(NCOL):
            o = jnp.dot(gated[...], wobuf[:, k * LANE : (k + 1) * LANE], preferred_element_type=F32).astype(BF16)
            turned = (k % NX) * NX + k // NX
            s["tbuf"][0][k * HALF : (k + 1) * HALF, :] = o[:HALF]
            s["tbuf"][1][turned * HALF : (turned + 1) * HALF, :] = o[HALF:]
            if k % 8 == 7:
                yield

        def give(f):
            def done(v):
                out[f * HALF : (f + 1) * HALF, :] = v.astype(BF16)

            return done

        gens = [xy_reduce(at, s["tbuf"][f], HALF, f, (8, 3), give(f), *s["ored_b" if f else "ored_a"]) for f in range(2)]
        yield from joint(*gens)

    for _ in joint(zchain(), forward(), backward(), lookup()):
        pass
    touched[...] = gring.total(pl.ds(OWN, CNT), 1)
    for h, lo, hi in ((0, 0, 528), (1, 528, OWN)):
        for a in range(lo, hi, 16):
            rows = pl.ds(a, 16)
            total[rows, :] = gring.total(rows, h)
    kring.flush()
    vring.flush()
    gring.flush()


def settle_kernel(step_of, rate, raw, total, touched, values, momentum, out, new_values, new_momentum):
    out[...] = raw[...]
    for p in range(LOCAL):
        f = jnp.exp(-(STEP - step_of[p]).astype(F32) * rate[...])
        hit = touched[p : p + 1, :] > 0.5
        v, m = values[p], momentum[p]
        m = jnp.where(hit, MOMENTUM_RATE * m + total[p] * f, m)
        new_momentum[p] = m
        new_values[p] = jnp.where(hit, v * f - LEARN_RATE * m, v)


def per_device(
    tokens,
    cotangent,
    query_weight,
    slot_keys,
    values,
    momentum,
    page_ids,
    last_step,
    decay_rate,
    gate_weight,
    out_weight,
):
    pids = page_ids.reshape(-1)
    code = (jnp.arange(PAIRS) * LOCAL + pids % LOCAL)[None, :]
    none = PAIRS * LOCAL

    def listed(owner, second):
        match = (pids // LOCAL)[None, :] == owner[:, None]
        first = jnp.min(jnp.where(match, code, none), axis=1)
        last = jnp.max(jnp.where(match, code, -1), axis=1)
        valid = jnp.where(second, last > first, first < none)
        return jnp.where(valid, jnp.where(second, last, first), 0), valid

    n = jnp.arange(2 * OWNERS)
    pair = listed(n // 2, n % 2 == 1)[0] // LOCAL
    n = jnp.arange(2 * OWNERS * LOCAL)
    both, valid = listed(n // (2 * LOCAL), n // LOCAL % 2 == 1)
    mark = (valid & (both % LOCAL == n % LOCAL)).astype(F32)
    paged = (LOCAL, PAGE, LANE)
    rate = decay_rate.reshape(1, LANE)
    stored = values.reshape(paged)
    raw, total, touched = pl.pallas_call(
        kernel,
        out_shape=(
            jax.ShapeDtypeStruct((ROWS, LANE), BF16),
            jax.ShapeDtypeStruct((OWN, LANE), F32),
            jax.ShapeDtypeStruct((CNT, LANE), F32),
        ),
        in_specs=[SM] * 5 + [ANY] * 4 + [VM] + [ANY] * 3,
        out_specs=(VM,) * 3,
        scratch_shapes=FLAT,
        compiler_params=pltpu.CompilerParams(collective_id=0, has_side_effects=True, vmem_limit_bytes=60 << 20),
    )(
        pids,
        pair,
        pair // PICKS,
        mark,
        last_step,
        slot_keys.reshape(paged),
        tokens,
        cotangent,
        stored,
        rate,
        query_weight,
        gate_weight,
        out_weight,
    )
    layer_out, new_values, new_momentum = pl.pallas_call(
        settle_kernel,
        out_shape=(
            jax.ShapeDtypeStruct((ROWS, LANE), BF16),
            jax.ShapeDtypeStruct(paged, F32),
            jax.ShapeDtypeStruct(paged, F32),
        ),
        in_specs=[SM] + [VM] * 6,
        out_specs=(VM,) * 3,
    )(last_step, rate, raw, total.reshape(paged), touched, stored, momentum.reshape(paged))
    return (layer_out, new_values.reshape(OWN, LANE), new_momentum.reshape(OWN, LANE))


def solution(mesh):
    in_specs = (
        P("tok", "col"),
        P("tok", "col"),
        P(None, "col"),
        P("tok", "col"),
        P("tok", "col"),
        P("tok", "col"),
        P("tok", None),
        P("tok"),
        P("col"),
        P(None, "col"),
        P("col", None),
    )
    out_specs = (P("tok", "col"), P("tok", "col"), P("tok", "col"))
    return jax.shard_map(
        per_device, mesh=mesh, in_specs=in_specs, out_specs=out_specs, check_vma=False
    )
```

```python
import jax
import jax.numpy as jnp
from jax import lax
from jax.experimental import pallas as pl
from jax.experimental.pallas import tpu as pltpu
from jax.sharding import PartitionSpec as P

KW = 2048
STEP = 64
MOMENTUM_RATE = 0.9
LEARN_RATE = 1.0

NZ = 16
NX = 4
NCOL = 16
ROWS = 768
NB = 12
PICKS = 4
PAIRS = NB * PICKS
BLK = 64
PAGE = 128
LANE = 128
LOCAL = 8
OWNERS = 2 * NZ
PAGES = OWNERS * LOCAL
OWN = 1024
SHARE = ROWS // NCOL
HALF = ROWS // 2
CNT = 16
GROWS = OWN + CNT
TSTART = 3
TPACE = ()
CSTART = 8
CPACE = (4,)
SETTLE = 4
MESH = pl.DeviceIdType.MESH
HOPS = ((8, 7), (7, 8))
VM = pl.BlockSpec(memory_space=pltpu.VMEM)
ANY = pl.BlockSpec(memory_space=pl.ANY)
SM = pl.BlockSpec(memory_space=pltpu.SMEM)
F32 = jnp.float32
BF16 = jnp.bfloat16


class Place:
    def __init__(self):
        self.tok = lax.axis_index("tok")
        self.col = lax.axis_index("col")
        self.z = self.tok // 2
        self.c = self.tok % 2
        self.x = self.col // NX
        self.y = self.col % NX
        self.sib = (self.zc(0, 1 - self.c), self.col)
        self.zn = ((self.zc(1, self.c), self.col), (self.zc(-1, self.c), self.col))

    def zc(self, dz, c):
        return ((self.z + dz + NZ) % NZ) * 2 + c

    def xy(self, dx, dy):
        return ((self.x + dx + NX) % NX) * NX + (self.y + dy + NX) % NX

    def peer(self, dx, dy):
        return (self.tok, self.xy(dx, dy))


def remote(src, dst, ssem, rsem, dev):
    return pltpu.make_async_remote_copy(
        src_ref=src, dst_ref=dst, send_sem=ssem, recv_sem=rsem, device_id=dev, device_id_type=MESH
    )


def greet(devices):
    barrier = pltpu.get_barrier_semaphore()
    for dev in devices:
        pl.semaphore_signal(barrier, inc=1, device_id=dev, device_id_type=MESH)
    pl.semaphore_wait(barrier, len(devices))


class Ring:
    def __init__(self, at, src, dst, rsend, rrecv, ssend, srecv, own):
        self.at, self.src, self.dst, self.own = at, src, dst, own
        self.ring, self.side = (rsend, rrecv), (ssend, srecv)
        self.sent = []

    def start(self, copy):
        copy.start()
        self.sent.append(copy)

    def block(self, d, h, s, core):
        return self.dst.at[pl.ds(self.at.zc(-s if d == 0 else s, core) * LOCAL + h * (LOCAL // 2), LOCAL // 2)]

    def hop(self, d, h, s):
        b = self.block(d, h, s, self.at.c)
        from_ = b if s else self.src.at[pl.ds(h * (LOCAL // 2), LOCAL // 2)]
        return remote(from_, b, self.ring[0].at[d, h, s], self.ring[1].at[d, h, s], self.at.zn[d])

    def across(self, d, h, s, core):
        b = self.block(d, h, s, core)
        return remote(b, b, self.side[0].at[d, h, s - 1], self.side[1].at[d, h, s - 1], self.at.sib)

    def whole(self):
        b = self.dst.at[pl.ds(self.at.zc(0, 1 - self.at.c) * LOCAL, LOCAL)]
        return remote(b, b, self.own.at[0], self.own.at[1], self.at.sib)

    def begin(self):
        for h in range(2):
            for d in range(2):
                self.start(self.hop(d, h, 0))
        b = self.dst.at[pl.ds(self.at.tok * LOCAL, LOCAL)]
        self.start(remote(self.src, b, self.own.at[0], self.own.at[1], self.at.sib))

    def step(self, s, h):
        for d in range(2):
            if s > HOPS[d][h]:
                continue
            b = self.block(d, h, s, self.at.c)
            remote(b, b, self.ring[0].at[d, h, s - 1], self.ring[1].at[d, h, s - 1], self.at.zn[d]).wait_recv()
            if s < HOPS[d][h]:
                self.start(self.hop(d, h, s))
            self.start(self.across(d, h, s, self.at.c))

    def finish(self):
        other = 1 - self.at.c
        self.whole().wait_recv()
        for s in range(1, 9):
            for h in range(2):
                for d in range(2):
                    if s <= HOPS[d][h]:
                        self.across(d, h, s, other).wait_recv()

    def flush(self):
        for copy in self.sent:
            copy.wait_send()


def xy_gather(at, src, dst, n, cut, sends, recvs, first):
    sent = []
    lo, hi = pl.ds(0, cut), pl.ds(cut, n - cut)

    def shift(a, b):
        return (a, b) if first == 0 else (b, a)

    def dev(a, b):
        return at.peer(*shift(a, b))

    def slot(a, b):
        return dst.at[pl.ds(pl.multiple_of(at.xy(*shift(a, b)) * n, n), n)]

    def start(block, k, to):
        copy = remote(block, block, sends.at[k], recvs.at[k], to)
        copy.start()
        sent.append(copy)

    def wait(block, k, to):
        remote(block, block, sends.at[k], recvs.at[k], to).wait_recv()

    for k, to in ((0, dev(1, 0)), (1, dev(-1, 0)), (4, dev(0, 1)), (5, dev(0, -1))):
        copy = remote(src, slot(0, 0), sends.at[k], recvs.at[k], to)
        copy.start()
        sent.append(copy)
    yield
    wait(slot(-1, 0), 0, dev(1, 0))
    start(slot(-1, 0).at[lo], 2, dev(1, 0))
    wait(slot(1, 0), 1, dev(-1, 0))
    start(slot(1, 0).at[hi], 3, dev(-1, 0))
    for item, a in ((1, -1), (2, 1)):
        start(slot(a, 0), 4 + 4 * item, dev(0, 1))
        start(slot(a, 0), 5 + 4 * item, dev(0, -1))
    yield
    wait(slot(2, 0).at[lo], 2, dev(1, 0))
    wait(slot(2, 0).at[hi], 3, dev(-1, 0))
    start(slot(2, 0), 4 + 4 * 3, dev(0, 1))
    start(slot(2, 0), 5 + 4 * 3, dev(0, -1))
    yield
    for item, a in ((0, 0), (1, -1), (2, 1), (3, 2)):
        k = 4 + 4 * item
        wait(slot(a, -1), k, dev(0, 1))
        start(slot(a, -1).at[lo], k + 2, dev(0, 1))
        wait(slot(a, 1), k + 1, dev(0, -1))
        start(slot(a, 1).at[hi], k + 3, dev(0, -1))
        yield
    for item, a in ((0, 0), (1, -1), (2, 1), (3, 2)):
        k = 4 + 4 * item
        wait(slot(a, 2).at[lo], k + 2, dev(0, 1))
        wait(slot(a, 2).at[hi], k + 3, dev(0, -1))
    for copy in sent:
        copy.wait_send()


def xy_spread(at, dst, n, sends, recvs, first, waits):
    sent = []

    def dev(a, b):
        return at.peer(a, b) if first == 0 else at.peer(b, a)

    def slot(a, b):
        i = at.xy(a, b) if first == 0 else at.xy(b, a)
        return dst.at[pl.ds(pl.multiple_of(i * n, n), n)]

    def start(block, k, to):
        copy = remote(block, block, sends.at[k], recvs.at[k], to)
        copy.start()
        sent.append(copy)

    def wait(block, k, to):
        remote(block, block, sends.at[k], recvs.at[k], to).wait_recv()

    line = (2, 1, -1)
    for k, a in enumerate(line):
        start(slot(0, 0), k, dev(a, 0))
    for k, b in enumerate(line):
        start(slot(0, 0), 3 + k, dev(0, b))
    for _ in range(waits[0]):
        yield
    for j, a in enumerate(line):
        wait(slot(-a, 0), j, dev(a, 0))
        for k, b in enumerate(line):
            start(slot(-a, 0), 6 + 3 * j + k, dev(0, b))
    for _ in range(waits[1]):
        yield
    for k, b in enumerate(line):
        wait(slot(0, -b), 3 + k, dev(0, b))
        for j, a in enumerate(line):
            wait(slot(-a, -b), 6 + 3 * j + k, dev(0, b))
    for copy in sent:
        copy.wait_send()


def xy_reduce(at, terms, n, first, waits, done, got1, part, got2, send1, recv1, send2, recv2):
    sent = []
    mine = (at.x, at.y) if first == 0 else (at.y, at.x)

    def dev(a, b):
        return at.peer(a, b) if first == 0 else at.peer(b, a)

    def line(i, size):
        return pl.ds(pl.multiple_of(((i + NX) % NX) * size, size), size)

    for k, a in enumerate((2, 1, -1)):
        copy = remote(terms.at[line(mine[0] + a, NX * n)], got1.at[k], send1.at[k], recv1.at[k], dev(a, 0))
        copy.start()
        sent.append(copy)
    for _ in range(waits[0]):
        yield
    for k, a in enumerate((2, 1, -1)):
        remote(got1.at[k], got1.at[k], send1.at[k], recv1.at[k], dev(a, 0)).wait_recv()

    def add(b, carry):
        v = terms[pl.ds(pl.multiple_of((mine[0] * NX + b) * n, n), n), :].astype(F32)
        rows = pl.ds(pl.multiple_of(b * n, n), n)
        for k in range(3):
            v = v + got1[k, rows, :].astype(F32)
        part[rows, :] = v.astype(part.dtype)
        return carry

    lax.fori_loop(0, NX, add, 0)
    for k, b in enumerate((2, 1, -1)):
        copy = remote(part.at[line(mine[1] + b, n)], got2.at[k], send2.at[k], recv2.at[k], dev(0, b))
        copy.start()
        sent.append(copy)
    for _ in range(waits[1]):
        yield
    for k, b in enumerate((2, 1, -1)):
        remote(got2.at[k], got2.at[k], send2.at[k], recv2.at[k], dev(0, b)).wait_recv()
    v = part[line(mine[1], n), :].astype(F32)
    for k in range(3):
        v = v + got2[k].astype(F32)
    done(v)
    for copy in sent:
        copy.wait_send()


def sub(h):
    return (0, 528, 176) if h == 0 else (528, 512, 128)


class RingSum:
    ORDER = (8, 7, -7, 6, -6, 5, -5, 4, -4, 3, -3, 2, -2, 1, -1, 0)

    def __init__(self, at, mine, theirs, stage, land, xsend, xrecv, rsend, rrecv):
        self.at, self.mine, self.theirs, self.stage, self.land = at, mine, theirs, stage, land
        self.side, self.ring = (xsend, xrecv), (rsend, rrecv)
        self.sent = []

    def give(self, off):
        copy = remote(
            self.mine.at[self.at.zc(off, 1 - self.at.c)],
            self.theirs.at[off + 7],
            self.side[0].at[off + 7],
            self.side[1].at[off + 7],
            self.at.sib,
        )
        copy.start()
        self.sent.append(copy)

    def wait_side(self, off):
        b = self.theirs.at[off + 7]
        remote(b, b, self.side[0].at[off + 7], self.side[1].at[off + 7], self.at.sib).wait_recv()

    def landed(self, d, h, s):
        first, size, tile = sub(h)
        b = self.land.at[d, s, pl.ds(first, size)]
        remote(b, b, self.ring[0].at[d, h, s], self.ring[1].at[d, h, s], self.at.zn[d]).wait_recv()

    def step(self, s, h):
        if h == 0:
            if s == 0:
                self.wait_side(8)
            if s < 7:
                self.wait_side(7 - s)
                self.wait_side(s - 7)
        first, size, tile = sub(h)
        for d in range(2):
            if s >= HOPS[d][h]:
                continue
            far = HOPS[d][h] - s
            off = far if d == 0 else -far
            buf = 8 if far == 8 else off
            owner = self.at.zc(off, self.at.c)
            if s:
                self.landed(d, h, s - 1)
            for t in range(size // tile):
                rows = pl.ds(first + t * tile, tile)
                v = self.mine[owner, rows, :].astype(F32) + self.theirs[buf + 7, rows, :].astype(F32)
                if s:
                    v = v + self.land[d, s - 1, rows, :].astype(F32)
                self.stage[d, s, rows, :] = v.astype(BF16)
            rows = pl.ds(first, size)
            copy = remote(
                self.stage.at[d, s, rows],
                self.land.at[d, s, rows],
                self.ring[0].at[d, h, s],
                self.ring[1].at[d, h, s],
                self.at.zn[d],
            )
            copy.start()
            self.sent.append(copy)

    def finish(self):
        self.wait_side(0)
        for h in range(2):
            for d in range(2):
                self.landed(d, h, HOPS[d][h] - 1)

    def total(self, rows, h):
        v = self.mine[self.at.tok, rows, :].astype(F32) + self.theirs[7, rows, :].astype(F32)
        for d in range(2):
            v = v + self.land[d, HOPS[d][h] - 1, rows, :].astype(F32)
        return v

    def flush(self):
        for copy in self.sent:
            copy.wait_send()


def dma(*shape):
    return pltpu.SemaphoreType.DMA(shape)


def vmem(dtype, *shape):
    return pltpu.VMEM(shape, dtype)


def paced(gen, waits):
    for i, _ in enumerate(gen):
        for _ in range(waits[i] if i < len(waits) else 1):
            yield


def joint(*gens):
    gens = list(gens)
    while gens:
        left = []
        for g in gens:
            try:
                next(g)
                left.append(g)
            except StopIteration:
                pass
        gens = left
        if gens:
            yield


RING_SEMS = [dma(2, 2, 8), dma(2, 2, 8), dma(2, 2, 8), dma(2, 2, 8), dma(2)]
RED_SEMS = [dma(3)] * 4

SCRATCH = dict(
    kbuf=[vmem(BF16, PAGES, PAGE, LANE)],
    vbuf=[vmem(BF16, PAGES, PAGE, LANE)],
    gbuf=[vmem(BF16, OWNERS, GROWS, LANE)],
    tbuf=[vmem(BF16, NCOL * HALF, LANE)] * 2,
    cbuf=[vmem(BF16, NCOL * HALF, LANE)] * 2,
    wqg=[vmem(BF16, KW, 2 * LANE)],
    wobuf=[vmem(BF16, LANE, KW)],
    wot=[vmem(BF16, KW, LANE)],
    stored=[vmem(F32, LOCAL, PAGE, LANE)],
    local=[dma(10)],
    qbuf=[vmem(BF16, ROWS, LANE)],
    act=[vmem(F32, ROWS, LANE)],
    grads=[vmem(BF16, NB, BLK, LANE)],
    gated=[vmem(BF16, ROWS, LANE)],
    scores=[vmem(F32, ROWS, 2 * LANE)] * 2,
    sums=[vmem(F32, SHARE, 2 * LANE)] * 2,
    wbuf=[vmem(BF16, ROWS, 2 * LANE)] * 2,
    wpick=[vmem(BF16, PAIRS, BLK, LANE)],
    sred_a=[vmem(F32, 3, NX * SHARE, 2 * LANE), vmem(F32, NX * SHARE, 2 * LANE), vmem(F32, 3, SHARE, 2 * LANE)] + RED_SEMS,
    sred_b=[vmem(F32, 3, NX * SHARE, 2 * LANE), vmem(F32, NX * SHARE, 2 * LANE), vmem(F32, 3, SHARE, 2 * LANE)] + RED_SEMS,
    ored_a=[vmem(BF16, 3, NX * HALF, LANE), vmem(BF16, NX * HALF, LANE), vmem(BF16, 3, HALF, LANE)] + RED_SEMS,
    ored_b=[vmem(BF16, 3, NX * HALF, LANE), vmem(BF16, NX * HALF, LANE), vmem(BF16, 3, HALF, LANE)] + RED_SEMS,
    gring=[
        vmem(BF16, NZ, GROWS, LANE),
        vmem(BF16, 2, 8, GROWS, LANE),
        vmem(BF16, 2, 8, GROWS, LANE),
        dma(16),
        dma(16),
        dma(2, 2, 8),
        dma(2, 2, 8),
    ],
    kring=RING_SEMS,
    vring=RING_SEMS,
    tsem=[dma(20)] * 4,
    csem=[dma(20)] * 4,
    wsem=[dma(15)] * 4,
)
NAMES = list(SCRATCH)
FLAT = [s for name in NAMES for s in SCRATCH[name]]


def kernel(pids, pair, block, mark, step_of, keys, tokens, cotangent, values, rate, wq, wg, wo, out, total, touched, *refs):
    refs = list(refs)
    s = {}
    for name in NAMES:
        n = len(SCRATCH[name])
        s[name], refs = refs[:n], refs[n:]
    (kbuf,), (vbuf,), (gbuf,), (wqg,), (qbuf,), (act,), (grads,), (gated,), (wpick,), (local,) = (
        s[n] for n in ("kbuf", "vbuf", "gbuf", "wqg", "qbuf", "act", "grads", "gated", "wpick", "local")
    )
    (wobuf,), (wot,), (stored,) = s["wobuf"], s["wot"], s["stored"]
    at = Place()
    flags = set()
    greet([at.zn[0], at.zn[1], at.sib] + [at.peer(a, 0) for a in (1, -1, 2)] + [at.peer(0, a) for a in (1, -1, 2)])

    def factor(p):
        return jnp.exp(-(STEP - step_of[p]).astype(F32) * rate[...])

    mine = pl.ds(at.tok * LOCAL, LOCAL)
    kring = Ring(at, keys, kbuf, *s["kring"])
    vring = Ring(at, vbuf.at[mine], vbuf, *s["vring"])
    places = pl.ds(pl.multiple_of(at.col * HALF, HALF), HALF)

    def fetch(k, src, dst):
        copy = pltpu.make_async_copy(src, dst, local.at[k])
        copy.start()
        return copy

    halves = (pl.ds(0, HALF), pl.ds(HALF, HALF))
    gring = RingSum(at, gbuf, *s["gring"])

    def zchain():
        kring.begin()
        yield
        got = fetch(0, keys, kbuf.at[mine]), fetch(1, values, stored)
        yield
        for step in range(1, 9):
            for h in range(2):
                kring.step(step, h)
                if (step, h) == (7, 1):
                    vring.begin()
                yield
                if (step, h) == (2, 0):
                    for copy in got:
                        copy.wait()
                    for p in range(LOCAL):
                        vbuf[at.tok * LOCAL + p] = (stored[p] * factor(p)).astype(BF16)
        kring.finish()
        flags.add("keys")
        yield
        for step in range(1, 9):
            for h in range(2):
                vring.step(step, h)
                if step >= 7 and 7 in flags and "begun" not in flags:
                    flags.add("begun")
                    gring.step(0, 0)
                    gring.step(0, 1)
                yield
        vring.finish()
        flags.add("values")
        while 7 not in flags:
            yield
        if "begun" not in flags:
            gring.step(0, 0)
            gring.step(0, 1)
            yield
        for step in range(1, 8):
            while 7 - step not in flags:
                yield
            for h in range(2):
                gring.step(step, h)
                yield
        gring.finish()

    def wide(buf, r):
        return jnp.concatenate(
            [buf[pl.ds(pl.multiple_of(k * HALF + r * 128, 128), 128), :] for k in range(NCOL)], axis=1
        )

    def forward():
        gens = [
            xy_gather(at, tokens.at[halves[f]], s["tbuf"][f], HALF, 192, *s["tsem"][2 * f : 2 * f + 2], f) for f in range(2)
        ]
        gathered = joint(*gens)
        next(gathered)
        got = [fetch(2 + f, tokens.at[halves[f]], s["tbuf"][f].at[places]) for f in range(2)]
        got.append(fetch(4, wq, wqg.at[:, pl.ds(0, LANE)]))
        got.append(fetch(5, wg, wqg.at[:, pl.ds(LANE, LANE)]))
        got.append(fetch(6, wo, wobuf))
        got += [fetch(7 + f, cotangent.at[halves[f]], s["cbuf"][f].at[places]) for f in range(2)]
        for _ in range(TSTART):
            yield
        yield from paced(gathered, TPACE)
        for copy in got:
            copy.wait()
        flags.add("tokens")
        for h in range(2):

            def tile(r, carry, h=h):
                both = jnp.dot(wide(s["tbuf"][h], r), wqg[...], preferred_element_type=F32)
                rows = pl.ds(pl.multiple_of(h * HALF + r * 128, 128), 128)
                qbuf[rows, :] = both[:, :LANE].astype(BF16)
                g = both[:, LANE:]
                act[rows, :] = g / (1.0 + jnp.exp(-g))
                return carry

            for r in range(3):
                lax.fori_loop(r, r + 1, tile, 0)
                yield
        wot[...] = wobuf[...].T
        yield
        flags.add("queries")

    def backward():
        for _ in range(CSTART):
            yield
        gens = [xy_gather(at, cotangent.at[halves[f]], s["cbuf"][f], HALF, 192, *s["csem"][2 * f : 2 * f + 2], f) for f in range(2)]
        yield from paced(joint(*gens), CPACE)
        while "queries" not in flags:
            yield
        for h in range(2):

            def tile(r, carry, h=h):
                g = jnp.dot(wide(s["cbuf"][h], r), wot[...], preferred_element_type=F32)
                rows = pl.ds(pl.multiple_of(h * HALF + r * 128, 128), 128)
                g = (g * act[rows, :]).astype(BF16)
                grads[h * (NB // 2) + 2 * r] = g[:BLK]
                grads[h * (NB // 2) + 2 * r + 1] = g[BLK:]
                return carry

            for lo, hi in ((0, 2), (2, 3)):
                lax.fori_loop(lo, hi, tile, 0)
                yield
        flags.add("backward")

    def lookup():
        while not {"keys", "queries"} <= flags:
            yield
        for b in range(NB):
            q = qbuf[b * BLK : (b + 1) * BLK, :]
            for i in range(PICKS):
                page = kbuf[pids[b * PICKS + i]]
                v = lax.dot_general(q, page, (((1,), (1,)), ((), ())), preferred_element_type=F32)
                lanes = slice((i % 2) * PAGE, (i % 2 + 1) * PAGE)
                r = 0
                while r < BLK:
                    row = b * BLK + r
                    j, o = row // SHARE, row % SHARE
                    size = min(SHARE - o, BLK - r)
                    spot = j if i < 2 else (j % NX) * NX + j // NX
                    s["scores"][i // 2][spot * SHARE + o : spot * SHARE + o + size, lanes] = v[r : r + size]
                    r += size
            if b % 6 == 5:
                yield

        def keep(f):
            def done(v):
                s["sums"][f][...] = v * (KW**-0.5)

            return done

        gens = [
            xy_reduce(at, s["scores"][f], SHARE, f, (3, 1), keep(f), *s["sred_b" if f else "sred_a"]) for f in range(2)
        ]
        yield from joint(*gens)
        left, right = s["sums"][0][...], s["sums"][1][...]
        top = jnp.maximum(jnp.max(left, axis=1, keepdims=True), jnp.max(right, axis=1, keepdims=True))
        left, right = jnp.exp(left - top), jnp.exp(right - top)
        total = jnp.sum(left, axis=1, keepdims=True) + jnp.sum(right, axis=1, keepdims=True)
        rows = pl.ds(pl.multiple_of(at.col * SHARE, SHARE), SHARE)
        s["wbuf"][0][rows, :] = (left / total).astype(BF16)
        s["wbuf"][1][rows, :] = (right / total).astype(BF16)
        gens = [xy_spread(at, s["wbuf"][f], SHARE, *s["wsem"][2 * f : 2 * f + 2], f, (2, 2)) for f in range(2)]
        yield from joint(*gens)
        for b in range(NB):
            for i in range(PICKS):
                lanes = slice((i % 2) * PAGE, (i % 2 + 1) * PAGE)
                wpick[b * PICKS + i] = s["wbuf"][i // 2][b * BLK : (b + 1) * BLK, lanes]
        flags.add("weights")
        while "backward" not in flags:
            yield
        for off in RingSum.ORDER:
            for core in range(2):
                owner = at.zc(off, core)
                found = []
                for k in range(2):
                    n = owner * 2 + k
                    v = lax.dot_general(
                        wpick[pair[n]], grads[block[n]], (((0,), (0,)), ((), ())), preferred_element_type=F32
                    )
                    found.append((v, [mark[n * LOCAL + p] for p in range(LOCAL)]))
                row = lax.broadcasted_iota(jnp.int32, (CNT, LANE), 0)
                count = jnp.zeros((CNT, LANE), F32)
                for p in range(LOCAL):
                    v = found[0][0] * found[0][1][p] + found[1][0] * found[1][1][p]
                    gbuf[owner, p * PAGE : (p + 1) * PAGE, :] = v.astype(BF16)
                    count = jnp.where(row == p, found[0][1][p] + found[1][1][p], count)
                gbuf[owner, OWN:, :] = count.astype(BF16)
            gring.give(off)
            if off <= 0:
                flags.add(-off)
                if off in (-7, -5, -3, -1, 0):
                    yield
        while "values" not in flags:
            yield

        def mix(b, carry):
            rows = pl.ds(pl.multiple_of(b * BLK, BLK), BLK)
            m = jnp.zeros((BLK, LANE), F32)
            for i in range(PICKS):
                n = b * PICKS + i
                m += jnp.dot(wpick[n], vbuf[pids[n]], preferred_element_type=F32)
            gated[rows, :] = (m * act[rows, :]).astype(BF16)
            return carry

        for b in (0, 6):
            lax.fori_loop(b, b + 6, mix, 0)
            yield
        for k in range(NCOL):
            o = jnp.dot(gated[...], wobuf[:, k * LANE : (k + 1) * LANE], preferred_element_type=F32).astype(BF16)
            turned = (k % NX) * NX + k // NX
            s["tbuf"][0][k * HALF : (k + 1) * HALF, :] = o[:HALF]
            s["tbuf"][1][turned * HALF : (turned + 1) * HALF, :] = o[HALF:]
            if k % 8 == 7:
                yield

        def give(f):
            def done(v):
                out[f * HALF : (f + 1) * HALF, :] = v.astype(BF16)

            return done

        gens = [xy_reduce(at, s["tbuf"][f], HALF, f, (8, 3), give(f), *s["ored_b" if f else "ored_a"]) for f in range(2)]
        yield from joint(*gens)

    for _ in joint(zchain(), forward(), backward(), lookup()):
        pass
    touched[...] = gring.total(pl.ds(OWN, CNT), 1)
    for h, lo, hi in ((0, 0, 528), (1, 528, OWN)):
        for a in range(lo, hi, 16):
            rows = pl.ds(a, 16)
            total[rows, :] = gring.total(rows, h)
    kring.flush()
    vring.flush()
    gring.flush()


def settle_kernel(step_of, rate, raw, total, touched, values, momentum, out, new_values, new_momentum):
    out[...] = raw[...]
    for p in range(LOCAL // SETTLE):
        page = pl.program_id(0) * (LOCAL // SETTLE) + p
        f = jnp.exp(-(STEP - step_of[page]).astype(F32) * rate[...])
        hit = touched[pl.ds(page, 1), :] > 0.5
        v, m = values[p], momentum[p]
        m = jnp.where(hit, MOMENTUM_RATE * m + total[p] * f, m)
        new_momentum[p] = m
        new_values[p] = jnp.where(hit, v * f - LEARN_RATE * m, v)


def per_device(
    tokens,
    cotangent,
    query_weight,
    slot_keys,
    values,
    momentum,
    page_ids,
    last_step,
    decay_rate,
    gate_weight,
    out_weight,
):
    pids = page_ids.reshape(-1)
    code = (jnp.arange(PAIRS) * LOCAL + pids % LOCAL)[None, :]
    none = PAIRS * LOCAL

    def listed(owner, second):
        match = (pids // LOCAL)[None, :] == owner[:, None]
        first = jnp.min(jnp.where(match, code, none), axis=1)
        last = jnp.max(jnp.where(match, code, -1), axis=1)
        valid = jnp.where(second, last > first, first < none)
        return jnp.where(valid, jnp.where(second, last, first), 0), valid

    n = jnp.arange(2 * OWNERS)
    pair = listed(n // 2, n % 2 == 1)[0] // LOCAL
    n = jnp.arange(2 * OWNERS * LOCAL)
    both, valid = listed(n // (2 * LOCAL), n // LOCAL % 2 == 1)
    mark = (valid & (both % LOCAL == n % LOCAL)).astype(F32)
    paged = (LOCAL, PAGE, LANE)
    rate = decay_rate.reshape(1, LANE)
    stored = values.reshape(paged)
    raw, total, touched = pl.pallas_call(
        kernel,
        out_shape=(
            jax.ShapeDtypeStruct((ROWS, LANE), BF16),
            jax.ShapeDtypeStruct((OWN, LANE), F32),
            jax.ShapeDtypeStruct((CNT, LANE), F32),
        ),
        in_specs=[SM] * 5 + [ANY] * 4 + [VM] + [ANY] * 3,
        out_specs=(VM,) * 3,
        scratch_shapes=FLAT,
        compiler_params=pltpu.CompilerParams(collective_id=0, has_side_effects=True, vmem_limit_bytes=60 << 20),
    )(
        pids,
        pair,
        pair // PICKS,
        mark,
        last_step,
        slot_keys.reshape(paged),
        tokens,
        cotangent,
        stored,
        rate,
        query_weight,
        gate_weight,
        out_weight,
    )
    rows = pl.BlockSpec((ROWS // SETTLE, LANE), lambda i: (i, 0))
    pages = pl.BlockSpec((LOCAL // SETTLE, PAGE, LANE), lambda i: (i, 0, 0))
    layer_out, new_values, new_momentum = pl.pallas_call(
        settle_kernel,
        out_shape=(
            jax.ShapeDtypeStruct((ROWS, LANE), BF16),
            jax.ShapeDtypeStruct(paged, F32),
            jax.ShapeDtypeStruct(paged, F32),
        ),
        grid=(SETTLE,),
        in_specs=[SM, VM, rows, pages, VM, pages, pages],
        out_specs=(rows, pages, pages),
    )(last_step, rate, raw, total.reshape(paged), touched, stored, momentum.reshape(paged))
    return (layer_out, new_values.reshape(OWN, LANE), new_momentum.reshape(OWN, LANE))


def solution(mesh):
    in_specs = (
        P("tok", "col"),
        P("tok", "col"),
        P(None, "col"),
        P("tok", "col"),
        P("tok", "col"),
        P("tok", "col"),
        P("tok", None),
        P("tok"),
        P("col"),
        P(None, "col"),
        P("col", None),
    )
    out_specs = (P("tok", "col"), P("tok", "col"), P("tok", "col"))
    return jax.shard_map(
        per_device, mesh=mesh, in_specs=in_specs, out_specs=out_specs, check_vma=False
    )
```
